32 devices in a mesh: seq: 8 (over z, x), ch: 4 (over y, core).
Axes of the slice: x: 2, y: 2, z: 4, core: 2. Of those that a mesh axis runs over, the one named last changes fastest.
Arguments:
- query_rows: float32 [4096, 2048], P('seq', 'ch'), may hold values from -6 to 6
- key_rows: float32 [4096, 2048], P('seq', 'ch'), may hold values from -6 to 6
- value_rows: float32 [4096, 2048], P('seq', 'ch'), may hold values from -6 to 6
- filters: float32 [4096, 2048], P('seq', 'ch'), may hold values from -0.09375 to 0.09375
- skip_gain: float32 [2048], P('ch'), may hold values from -4 to 4
- out_weight: float32 [2048, 2048], P('ch'), may hold values from -0.125 to 0.125
Outputs:
- projected: float32 [2048, 4096], P('ch', 'seq')
The draws below stay inside these ranges and needn't reach their ends.
All inputs are finite; a program needn't handle non-finite values.
Results may differ from the reference program's by a relative error of at most 0.00007.
Values sent between devices are 32-bit elements; how exact they have to be, the bound alone decides.
No kernel may reach another device: no remote copies, remote signals or barrier semaphores. Data moves between devices by JAX's collectives and lax.ppermute only.
A program may use at most 64 MiB of HBM per device.

```python
import jax
import jax.numpy as jnp
from jax import lax

C = 2048
SEQ = 4096


def shard_levels(rng, shape, shards, least, top_value):
    def one(dim, parts):
        draws = jax.random.uniform(jax.random.fold_in(jax.random.fold_in(rng, 6), dim), (parts,), jnp.float32, least / len(shards), top_value / len(shards))
        return jnp.repeat(jnp.exp(draws), shape[dim] // parts).reshape((-1,) + (1,) * (len(shape) - dim - 1))

    gain = one(*shards[0])
    for cut in shards[1:]:
        gain = gain * one(*cut)
    return gain


def centred(own_key, dims, scale, reach, split=(), kind=jnp.bfloat16):
    array = scale * jax.random.normal(own_key, dims, jnp.float32)
    if split:
        array = array * shard_levels(own_key, dims, split, -0.22, 0.18)
    return jnp.clip(array, -reach, reach).astype(kind)


def setup_inputs(seed: int = 0) -> dict:
    seeds = jax.random.split(jax.random.key(seed), 7)
    query_rows = centred(seeds[0], (SEQ, C), 1.0, 6.0, ((0, 8), (1, 4)), jnp.float32)
    key_rows = centred(seeds[1], (SEQ, C), 1.0, 6.0, ((0, 8), (1, 4)), jnp.float32)
    value_rows = centred(seeds[2], (SEQ, C), 1.0, 6.0, ((0, 8), (1, 4)), jnp.float32)
    filters = centred(seeds[3], (SEQ, C), SEQ ** -0.5, 0.09375, ((0, 8), (1, 4)), jnp.float32)
    skip_gain = centred(seeds[4], (C,), 1.0, 4.0, ((0, 4),), jnp.float32)
    out_weight = centred(seeds[5], (C, C), C ** -0.5, 0.125, ((0, 4),), jnp.float32)
    return dict(query_rows=query_rows, key_rows=key_rows, value_rows=value_rows, filters=filters, skip_gain=skip_gain, out_weight=out_weight)


def reference(query_rows, key_rows, value_rows, filters, skip_gain, out_weight):
    gated = key_rows * value_rows
    period = 2 * SEQ
    spectrum = jnp.fft.rfft(gated, n=period, axis=0) * jnp.fft.rfft(filters, n=period, axis=0)
    convolved = jnp.fft.irfft(spectrum, n=period, axis=0)[:SEQ].astype(gated.dtype)
    mixed = query_rows * (convolved + skip_gain[None, :] * gated)
    return jnp.dot(out_weight.T, mixed.T, precision=lax.Precision.HIGHEST, preferred_element_type=jnp.float32)
```

```python
import functools
import math

import jax
import jax.numpy as jnp
import ml_dtypes
import numpy as np
from jax import lax
from jax.experimental import pallas as pl
from jax.experimental.pallas import tpu as pltpu
from jax.sharding import PartitionSpec as P

LANES = 128
VMEM_BYTES = 56 * 1024 * 1024
CHUNKS = 1

f32 = jnp.float32
bf16 = jnp.bfloat16


def halves(x):
    high = x.astype(bf16)
    return high, (x - high.astype(f32)).astype(bf16)


def dot(a, b):
    return jnp.dot(a, b, preferred_element_type=f32)


def dot_split(a_high, a_low, b_high, b_low):
    return dot(a_high, b_high) + (dot(a_low, b_high) + dot(a_high, b_low))


def split_table(table):
    high = table.astype(np.float32).astype(ml_dtypes.bfloat16)
    low = (table - high.astype(np.float64)).astype(np.float32).astype(ml_dtypes.bfloat16)
    return jnp.asarray(high), jnp.asarray(low)


def transforms(length):
    orders = np.concatenate([np.arange(0, length, 2), np.arange(1, length, 2)])
    angle = math.pi / length * (orders[None, :] + 0.5) * np.arange(length)[:, None]
    forward = np.concatenate([np.cos(angle), -np.sin(angle)], axis=1)
    return split_table(forward), split_table(forward.T / length)


def call(body, out_shape, *, grid_spec=None, in_specs=None, out_specs=None, scratch=(), flops=0, size=0, aliases=None):
    params = pltpu.CompilerParams(vmem_limit_bytes=VMEM_BYTES)
    cost = pl.CostEstimate(flops=flops, bytes_accessed=size, transcendentals=0)
    kwargs = dict(out_shape=out_shape, compiler_params=params, cost_estimate=cost)
    if aliases:
        kwargs["input_output_aliases"] = aliases
    if grid_spec is not None:
        return pl.pallas_call(body, grid_spec=grid_spec, **kwargs)
    return pl.pallas_call(body, in_specs=in_specs, out_specs=out_specs, scratch_shapes=list(scratch), **kwargs)


def pack_body(group, slim, chunks, me_ref, key_ref, value_ref, filter_ref, *rest):
    outs, (gated, taps) = rest[:-2], rest[-2:]
    part = slim // chunks
    gated[...] = (key_ref[...] * value_ref[...]).T
    taps[...] = filter_ref[...].T
    low = lax.rem(me_ref[0], group)
    for e in range(group):
        start = jnp.bitwise_xor(low, e) * slim
        for k in range(chunks):
            rows = pl.ds(pl.multiple_of(start + k * part, 8), part)
            out = outs[e * chunks + k]
            out[0:part, :] = gated[rows, :]
            out[part : 2 * part, :] = taps[rows, :]


def pack(me, key_rows, value_rows, filters, t, group, slim, chunks):
    length = key_rows.shape[0]
    part = slim // chunks
    block = pl.BlockSpec((length, LANES), lambda i, me_ref: (0, jnp.bitwise_xor(me_ref[0] // group, t)))
    spec = pl.BlockSpec((2 * part, length), lambda i, me_ref: (0, 0))
    count = group * chunks
    return call(
        functools.partial(pack_body, group, slim, chunks),
        [jax.ShapeDtypeStruct((2 * part, length), f32)] * count,
        grid_spec=pltpu.PrefetchScalarGridSpec(
            num_scalar_prefetch=1,
            grid=(1,),
            in_specs=[block] * 3,
            out_specs=[spec] * count,
            scratch_shapes=[pltpu.VMEM((LANES, length), f32)] * 2,
        ),
        flops=length * LANES * 64,
        size=5 * length * LANES * 4,
    )(me, key_rows, value_rows, filters)


def conv_body(count, me_ref, fwd_high, fwd_low, inv_high, inv_low, *rest):
    arrived = rest[:count]
    outs = rest[count : 2 * count]
    spectra, totals = rest[2 * count :]
    me = me_ref[0]
    part = arrived[0].shape[0] // 2
    length = arrived[0].shape[1]
    rows = jnp.concatenate([ref[...] for ref in arrived], axis=0)
    high, low = halves(rows)
    result = dot_split(high, low, fwd_high[...], fwd_low[...])
    for s in range(count):
        spectra[jnp.bitwise_xor(me, s)] = result[s * 2 * part : (s + 1) * 2 * part]

    lane_steps = length // LANES

    def tile(index, carry):
        group = index // lane_steps
        lane = lax.rem(index, lane_steps)
        sign = jnp.where(lane * 2 < lane_steps, 1.0, -1.0).astype(f32)
        top = pl.ds(pl.multiple_of(group * 8, 8), 8)
        bottom = pl.ds(pl.multiple_of(part + group * 8, 8), 8)
        re = pl.ds(pl.multiple_of(lane * LANES, LANES), LANES)
        im = pl.ds(pl.multiple_of(length + lane * LANES, LANES), LANES)
        gated_re = [spectra[p, top, re] for p in range(count)]
        gated_im = [spectra[p, top, im] for p in range(count)]
        taps_re, taps_im = [], []
        last_re = last_im = None
        for q in range(count):
            now_re, now_im = spectra[q, bottom, re], spectra[q, bottom, im]
            if q == 0:
                taps_re.append(now_re)
                taps_im.append(now_im)
            else:
                taps_re.append(now_re - sign * last_im)
                taps_im.append(now_im + sign * last_re)
            last_re, last_im = now_re, now_im
        for i in range(count):
            total_re = total_im = None
            for p in range(i + 1):
                a_re, a_im = gated_re[p], gated_im[p]
                b_re, b_im = taps_re[i - p], taps_im[i - p]
                one_re = a_re * b_re - a_im * b_im
                one_im = a_re * b_im + a_im * b_re
                total_re = one_re if p == 0 else total_re + one_re
                total_im = one_im if p == 0 else total_im + one_im
            totals[i, top, re] = total_re
            totals[i, top, im] = total_im
        return carry

    lax.fori_loop(0, part // 8 * lane_steps, tile, 0)

    stacked = jnp.concatenate([totals[jnp.bitwise_xor(me, s)] for s in range(count)], axis=0)
    high, low = halves(stacked)
    result = dot_split(high, low, inv_high[...], inv_low[...])
    for s in range(count):
        outs[s][...] = result[s * part : (s + 1) * part]


def convolve(me, arrived, forward, inverse):
    count = len(arrived)
    double, length = arrived[0].shape
    part = double // 2
    vmem = pl.BlockSpec(memory_space=pltpu.VMEM)
    return call(
        functools.partial(conv_body, count),
        [jax.ShapeDtypeStruct((part, length), f32)] * count,
        in_specs=[pl.BlockSpec(memory_space=pltpu.SMEM)] + [vmem] * (4 + count),
        out_specs=[vmem] * count,
        scratch=[
            pltpu.VMEM((count, double, 2 * length), f32),
            pltpu.VMEM((count, part, 2 * length), f32),
        ],
        flops=6 * count * double * length * 3 * length,
        size=8 * length * length * 2 + count * double * length * 6,
    )(me, *forward, *inverse, *arrived)


def gates_body(count, chunks, me_ref, query_ref, key_ref, value_ref, skip_ref, gate_ref, direct_ref, gate_t, direct_t):
    query = query_ref[...]
    gate_t[...] = query.T
    direct_t[...] = (query * (skip_ref[...] * (key_ref[...] * value_ref[...]))).T
    slim = gate_t.shape[0] // count
    part = slim // chunks
    for k in range(chunks):
        for s in range(count):
            start = jnp.bitwise_xor(me_ref[0], s) * slim + k * part
            source = pl.ds(pl.multiple_of(start, 8), part)
            here = pl.ds((k * count + s) * part, part)
            gate_ref[here, :] = gate_t[source, :]
            direct_ref[here, :] = direct_t[source, :]


def gates(me, query_rows, key_rows, value_rows, skip_gain, count, chunks):
    length, channels = query_rows.shape
    vmem = pl.BlockSpec(memory_space=pltpu.VMEM)
    return call(
        functools.partial(gates_body, count, chunks),
        [jax.ShapeDtypeStruct((channels, length), f32)] * 2,
        in_specs=[pl.BlockSpec(memory_space=pltpu.SMEM)] + [vmem] * 4,
        out_specs=[vmem] * 2,
        scratch=[pltpu.VMEM((channels, length), f32)] * 2,
        flops=length * channels * 64,
        size=5 * length * channels * 4,
    )(me, query_rows, key_rows, value_rows, skip_gain[None, :])


def mix_body(*refs):
    count = (len(refs) - 1) // 3
    out = refs[-1]
    part = refs[0].shape[0]
    for e in range(count):
        out[e * part : (e + 1) * part, :] = refs[count + e][...] * refs[e][...] + refs[2 * count + e][...]


def mix(pieces, gate, direct, first):
    part, length = pieces[0].shape
    count = len(pieces)

    def rows(e):
        return pl.BlockSpec((part, length), lambda i: (first + e, 0))

    whole = pl.BlockSpec((part, length), lambda i: (0, 0))
    return call(
        mix_body,
        jax.ShapeDtypeStruct((count * part, length), f32),
        grid_spec=pl.GridSpec(
            grid=(1,),
            in_specs=[whole] * count + [rows(e) for e in range(count)] * 2,
            out_specs=pl.BlockSpec((count * part, length), lambda i: (0, 0)),
        ),
        flops=2 * count * part * length,
        size=4 * count * part * length * 4,
    )(*pieces, *[gate] * count, *[direct] * count)


def weights_body(count, chunks, me_ref, weight_ref, high_ref, low_ref, ordered):
    slim = ordered.shape[0] // count
    part = slim // chunks
    for k in range(chunks):
        for s in range(count):
            start = jnp.bitwise_xor(me_ref[0], s) * slim + k * part
            ordered[pl.ds((k * count + s) * part, part), :] = weight_ref[pl.ds(pl.multiple_of(start, 8), part), :]
    high, low = halves(ordered[...].T)
    high_ref[...] = high
    low_ref[...] = low


def weights(me, block, count, chunks):
    channels, width = block.shape
    vmem = pl.BlockSpec(memory_space=pltpu.VMEM)
    return call(
        functools.partial(weights_body, count, chunks),
        [jax.ShapeDtypeStruct((width, channels), bf16)] * 2,
        in_specs=[pl.BlockSpec(memory_space=pltpu.SMEM), vmem],
        out_specs=[vmem] * 2,
        scratch=[pltpu.VMEM((channels, width), f32)],
        flops=channels * width * 64,
        size=channels * width * 8,
    )(me, block)


def project_body(count, started, *refs):
    mixed, highs, lows = refs[:count], refs[count : 2 * count], refs[2 * count : 3 * count]
    out = refs[-1]
    rows = jnp.concatenate([ref[...] for ref in mixed], axis=0)
    high, low = halves(rows)
    w_high = jnp.concatenate([ref[...] for ref in highs], axis=1)
    w_low = jnp.concatenate([ref[...] for ref in lows], axis=1)
    total = dot_split(w_high, w_low, high, low)
    if started:
        total = total + refs[3 * count][...]
    out[...] = total


def project(mixed, tables, first, total):
    count = len(mixed)
    depth, length = mixed[0].shape
    width = tables[0][0].shape[0]
    whole = pl.BlockSpec((depth, length), lambda i: (0, 0))
    columns = pl.BlockSpec((width, depth), lambda i: (0, first))
    result = pl.BlockSpec((width, length), lambda i: (0, 0))
    started = total is not None
    return call(
        functools.partial(project_body, count, started),
        jax.ShapeDtypeStruct((width, length), f32),
        grid_spec=pl.GridSpec(
            grid=(1,),
            in_specs=[whole] * count + [columns] * (2 * count) + [result] * started,
            out_specs=result,
        ),
        flops=6 * count * depth * width * length,
        size=count * depth * (width + length) * 4 + 2 * width * length * 4,
        aliases={3 * count: 0} if started else None,
    )(*mixed, *[t[0] for t in tables], *[t[1] for t in tables], *([total] * started))


def swap(x, axis, size, offset):
    return lax.ppermute(x, axis, [(j, j ^ offset) for j in range(size)])


def per_device(query_rows, key_rows, value_rows, filters, skip_gain, out_weight):
    count = lax.axis_size("seq")
    peers = lax.axis_size("ch")
    length, channels = query_rows.shape
    slim = channels // count
    chunks = max(1, min(CHUNKS, slim // 8))
    group = LANES // slim
    width = out_weight.shape[1] // peers
    me = lax.axis_index("seq").astype(jnp.int32).reshape(1)
    mine = lax.axis_index("ch")
    forward, inverse = transforms(length)

    sent = [[None] * count for _ in range(chunks)]
    for t in reversed(range(count // group)):
        pieces = pack(me, key_rows, value_rows, filters, t, group, slim, chunks)
        for e in range(group):
            for k in range(chunks):
                sent[k][t * group + e] = pieces[e * chunks + k]
    arrived = [[None] * count for _ in range(chunks)]
    for k in range(chunks):
        for s in reversed(range(count)):
            arrived[k][s] = swap(sent[k][s], "seq", count, s) if s else sent[k][0]

    tables = []
    for o in range(peers):
        block = lax.dynamic_slice_in_dim(out_weight, (mine ^ o) * width, width, axis=1)
        tables.append(weights(me, swap(block, "ch", peers, o) if o else block, count, chunks))
    gate, direct = gates(me, query_rows, key_rows, value_rows, skip_gain, count, chunks)

    total = None
    for k in range(chunks):
        pieces = convolve(me, arrived[k], forward, inverse)
        back = [None] * count
        for s in reversed(range(count)):
            back[s] = swap(pieces[s], "seq", count, s) if s else pieces[0]
        units = 2
        step = count // units
        for u in range(units):
            first = u * step
            rows = mix(back[first : first + step], gate, direct, k * count + first)
            have = {0: rows}
            bit = peers // 2
            while bit:
                for o in list(have):
                    have[o | bit] = swap(have[o], "ch", peers, bit)
                bit //= 2
            order = sorted(have)
            total = project([have[o] for o in order], [tables[o] for o in order], k * units + u, total)
    return total


def solution(mesh):
    in_specs = (
        P("seq", "ch"),
        P("seq", "ch"),
        P("seq", "ch"),
        P("seq", "ch"),
        P("ch"),
        P("ch", None),
    )
    out_specs = P("ch", "seq")
    return jax.shard_map(
        per_device, mesh=mesh, in_specs=in_specs, out_specs=out_specs, check_vma=False
    )
```

```python
import functools
import math

import jax
import jax.numpy as jnp
import ml_dtypes
import numpy as np
from jax import lax
from jax.experimental import pallas as pl
from jax.experimental.pallas import tpu as pltpu
from jax.sharding import PartitionSpec as P

LANES = 128
MIB = 1024 * 1024
CHUNKS = 1

f32 = jnp.float32
bf16 = jnp.bfloat16


def halves(x):
    high = x.astype(bf16)
    return high, (x - high.astype(f32)).astype(bf16)


def dot(a, b):
    return jnp.dot(a, b, preferred_element_type=f32)


def dot_split(a_high, a_low, b_high, b_low):
    return dot(a_high, b_high) + (dot(a_low, b_high) + dot(a_high, b_low))


def split_table(table):
    high = table.astype(np.float32).astype(ml_dtypes.bfloat16)
    low = (table - high.astype(np.float64)).astype(np.float32).astype(ml_dtypes.bfloat16)
    return jnp.asarray(high), jnp.asarray(low)


def transforms(length):
    orders = np.concatenate([np.arange(0, length, 2), np.arange(1, length, 2)])
    angle = math.pi / length * (orders[None, :] + 0.5) * np.arange(length)[:, None]
    forward = np.concatenate([np.cos(angle), -np.sin(angle)], axis=1)
    return split_table(forward), split_table(forward.T / length)


def call(body, out_shape, *, grid_spec=None, in_specs=None, out_specs=None, scratch=(), room=16, aliases=None, work=1):
    params = pltpu.CompilerParams(vmem_limit_bytes=room * MIB)
    cost = pl.CostEstimate(flops=work, bytes_accessed=1, transcendentals=0)
    kwargs = dict(out_shape=out_shape, compiler_params=params, cost_estimate=cost)
    if aliases:
        kwargs["input_output_aliases"] = aliases
    if grid_spec is not None:
        return pl.pallas_call(body, grid_spec=grid_spec, **kwargs)
    return pl.pallas_call(body, in_specs=in_specs, out_specs=out_specs, scratch_shapes=list(scratch), **kwargs)


def pack_body(group, slim, chunks, me_ref, key_ref, value_ref, filter_ref, *rest):
    outs, (gated, taps) = rest[:-2], rest[-2:]
    part = slim // chunks
    gated[...] = (key_ref[...] * value_ref[...]).T
    taps[...] = filter_ref[...].T
    low = lax.rem(me_ref[0], group)
    for e in range(group):
        start = jnp.bitwise_xor(low, e) * slim
        for k in range(chunks):
            rows = pl.ds(pl.multiple_of(start + k * part, 8), part)
            out = outs[e * chunks + k]
            out[0:part, :] = gated[rows, :]
            out[part : 2 * part, :] = taps[rows, :]


def pack(me, key_rows, value_rows, filters, t, group, slim, chunks, room):
    length = key_rows.shape[0]
    part = slim // chunks
    block = pl.BlockSpec((length, LANES), lambda i, me_ref: (0, jnp.bitwise_xor(me_ref[0] // group, t)))
    spec = pl.BlockSpec((2 * part, length), lambda i, me_ref: (0, 0))
    count = group * chunks
    return call(
        functools.partial(pack_body, group, slim, chunks),
        [jax.ShapeDtypeStruct((2 * part, length), f32)] * count,
        grid_spec=pltpu.PrefetchScalarGridSpec(
            num_scalar_prefetch=1,
            grid=(1,),
            in_specs=[block] * 3,
            out_specs=[spec] * count,
            scratch_shapes=[pltpu.VMEM((LANES, length), f32)] * 2,
        ),
        room=room,
    )(me, key_rows, value_rows, filters)


def spectrum_body(*refs):
    arrived, (fwd_high, fwd_low), out = refs[:-3], refs[-3:-1], refs[-1]
    rows = jnp.concatenate([ref[...] for ref in arrived], axis=0)
    high, low = halves(rows)
    out[...] = dot_split(high, low, fwd_high[...], fwd_low[...])


def spectrum(arrived, forward):
    double, length = arrived[0].shape
    vmem = pl.BlockSpec(memory_space=pltpu.VMEM)
    return call(
        spectrum_body,
        jax.ShapeDtypeStruct((len(arrived) * double, 2 * length), f32),
        in_specs=[vmem] * (2 + len(arrived)),
        out_specs=vmem,
        room=16,
    )(*arrived, *forward)


def products(count, part, length, spectra, totals):
    lane_steps = length // LANES

    def tile(index, carry):
        group = index // lane_steps
        lane = lax.rem(index, lane_steps)
        sign = jnp.where(lane * 2 < lane_steps, 1.0, -1.0).astype(f32)
        top = pl.ds(pl.multiple_of(group * 8, 8), 8)
        bottom = pl.ds(pl.multiple_of(part + group * 8, 8), 8)
        re = pl.ds(pl.multiple_of(lane * LANES, LANES), LANES)
        im = pl.ds(pl.multiple_of(length + lane * LANES, LANES), LANES)
        gated_re = [spectra[p, top, re] for p in range(count)]
        gated_im = [spectra[p, top, im] for p in range(count)]
        taps_re, taps_im = [], []
        last_re = last_im = None
        for q in range(count):
            now_re, now_im = spectra[q, bottom, re], spectra[q, bottom, im]
            if q == 0:
                taps_re.append(now_re)
                taps_im.append(now_im)
            else:
                taps_re.append(now_re - sign * last_im)
                taps_im.append(now_im + sign * last_re)
            last_re, last_im = now_re, now_im
        for i in range(count):
            total_re = total_im = None
            for p in range(i + 1):
                a_re, a_im = gated_re[p], gated_im[p]
                b_re, b_im = taps_re[i - p], taps_im[i - p]
                one_re = a_re * b_re - a_im * b_im
                one_im = a_re * b_im + a_im * b_re
                total_re = one_re if p == 0 else total_re + one_re
                total_im = one_im if p == 0 else total_im + one_im
            totals[i, top, re] = total_re
            totals[i, top, im] = total_im
        return carry

    lax.fori_loop(0, part // 8 * lane_steps, tile, 0)


def conv_body(early, late, me_ref, fwd_high, fwd_low, inv_high, inv_low, near, *rest):
    arrived = rest[: len(late)]
    outs = rest[len(late) : 2 * len(late)]
    left, spectra, totals = rest[2 * len(late) :]
    count = len(early) + len(late)
    me = me_ref[0]
    double, length = arrived[0].shape
    part = double // 2
    for e, s in enumerate(early):
        spectra[jnp.bitwise_xor(me, s)] = near[e * double : (e + 1) * double, :]
    rows = jnp.concatenate([ref[...] for ref in arrived], axis=0)
    high, low = halves(rows)
    result = dot_split(high, low, fwd_high[...], fwd_low[...])
    for e, s in enumerate(late):
        spectra[jnp.bitwise_xor(me, s)] = result[e * double : (e + 1) * double]
    products(count, part, length, spectra, totals)
    stacked = jnp.concatenate([totals[jnp.bitwise_xor(me, s)] for s in late], axis=0)
    high, low = halves(stacked)
    result = dot_split(high, low, inv_high[...], inv_low[...])
    for e in range(len(late)):
        outs[e][...] = result[e * part : (e + 1) * part]
    for e, s in enumerate(early):
        left[e * part : (e + 1) * part, :] = totals[jnp.bitwise_xor(me, s)]


def convolve(me, early, late, near, arrived, forward, inverse):
    count = len(early) + len(late)
    double, length = arrived[0].shape
    part = double // 2
    vmem = pl.BlockSpec(memory_space=pltpu.VMEM)
    return call(
        functools.partial(conv_body, early, late),
        [jax.ShapeDtypeStruct((part, length), f32)] * len(late)
        + [jax.ShapeDtypeStruct((len(early) * part, 2 * length), f32)],
        in_specs=[pl.BlockSpec(memory_space=pltpu.SMEM)] + [vmem] * (5 + len(late)),
        out_specs=[vmem] * (len(late) + 1),
        scratch=[
            pltpu.VMEM((count, double, 2 * length), f32),
            pltpu.VMEM((count, part, 2 * length), f32),
        ],
        room=24,
    )(me, *forward, *inverse, near, *arrived)


def restore_body(left, inv_high, inv_low, *outs):
    part = outs[0].shape[0]
    high, low = halves(left[...])
    result = dot_split(high, low, inv_high[...], inv_low[...])
    for e, out in enumerate(outs):
        out[...] = result[e * part : (e + 1) * part]


def restore(left, inverse, pieces):
    rows, width = left.shape
    vmem = pl.BlockSpec(memory_space=pltpu.VMEM)
    return call(
        restore_body,
        [jax.ShapeDtypeStruct((rows // pieces, width // 2), f32)] * pieces,
        in_specs=[vmem] * 3,
        out_specs=[vmem] * pieces,
        room=16,
    )(left, *inverse)


def gates_body(count, chunks, me_ref, query_ref, key_ref, value_ref, skip_ref, gate_ref, direct_ref, gate_t, direct_t):
    query = query_ref[...]
    gate_t[...] = query.T
    direct_t[...] = (query * (skip_ref[...] * (key_ref[...] * value_ref[...]))).T
    slim = gate_t.shape[0] // count
    part = slim // chunks
    for k in range(chunks):
        for s in range(count):
            start = jnp.bitwise_xor(me_ref[0], s) * slim + k * part
            source = pl.ds(pl.multiple_of(start, 8), part)
            here = pl.ds((k * count + s) * part, part)
            gate_ref[here, :] = gate_t[source, :]
            direct_ref[here, :] = direct_t[source, :]


def gates(me, query_rows, key_rows, value_rows, skip_gain, count, chunks):
    length, channels = query_rows.shape
    vmem = pl.BlockSpec(memory_space=pltpu.VMEM)
    return call(
        functools.partial(gates_body, count, chunks),
        [jax.ShapeDtypeStruct((channels, length), f32)] * 2,
        in_specs=[pl.BlockSpec(memory_space=pltpu.SMEM)] + [vmem] * 4,
        out_specs=[vmem] * 2,
        scratch=[pltpu.VMEM((channels, length), f32)] * 2,
        room=16,
        work=10**12,
    )(me, query_rows, key_rows, value_rows, skip_gain[None, :])


def mix_body(*refs):
    count = (len(refs) - 1) // 3
    out = refs[-1]
    part = refs[0].shape[0]
    for e in range(count):
        out[e * part : (e + 1) * part, :] = refs[count + e][...] * refs[e][...] + refs[2 * count + e][...]


def mix(pieces, gate, direct, first):
    part, length = pieces[0].shape
    count = len(pieces)

    def rows(e):
        return pl.BlockSpec((part, length), lambda i: (first + e, 0))

    whole = pl.BlockSpec((part, length), lambda i: (0, 0))
    return call(
        mix_body,
        jax.ShapeDtypeStruct((count * part, length), f32),
        grid_spec=pl.GridSpec(
            grid=(1,),
            in_specs=[whole] * count + [rows(e) for e in range(count)] * 2,
            out_specs=pl.BlockSpec((count * part, length), lambda i: (0, 0)),
        ),
        room=16,
    )(*pieces, *[gate] * count, *[direct] * count)


def cut_body(weight_ref, out_ref):
    out_ref[0] = weight_ref[...]


def cut(out_weight, peers):
    channels, total = out_weight.shape
    width = total // peers
    return call(
        cut_body,
        jax.ShapeDtypeStruct((peers, channels, width), f32),
        grid_spec=pl.GridSpec(
            grid=(peers,),
            in_specs=[pl.BlockSpec((channels, width), lambda o: (0, o))],
            out_specs=pl.BlockSpec((1, channels, width), lambda o: (o, 0, 0)),
        ),
        room=56,
    )(out_weight)


def weights_body(count, chunks, me_ref, mine_ref, weight_ref, high_ref, low_ref, ordered):
    slim = ordered.shape[0] // count
    part = slim // chunks
    for k in range(chunks):
        for s in range(count):
            start = jnp.bitwise_xor(me_ref[0], s) * slim + k * part
            ordered[pl.ds((k * count + s) * part, part), :] = weight_ref[0, pl.ds(pl.multiple_of(start, 8), part), :]
    high, low = halves(ordered[...].T)
    high_ref[...] = high
    low_ref[...] = low


def weights(me, mine, blocks, count, chunks):
    peers, channels, width = blocks.shape
    result = pl.BlockSpec((width, channels), lambda o, me_ref, mine_ref: (0, o))
    return call(
        functools.partial(weights_body, count, chunks),
        [jax.ShapeDtypeStruct((width, peers * channels), bf16)] * 2,
        grid_spec=pltpu.PrefetchScalarGridSpec(
            num_scalar_prefetch=2,
            grid=(peers,),
            in_specs=[pl.BlockSpec((1, channels, width), lambda o, me_ref, mine_ref: (jnp.bitwise_xor(mine_ref[0], o), 0, 0))],
            out_specs=[result] * 2,
            scratch_shapes=[pltpu.VMEM((channels, width), f32)],
        ),
        room=12,
        work=10**12,
    )(me, mine, blocks)


def project_body(count, started, *refs):
    mixed, highs, lows = refs[:count], refs[count : 2 * count], refs[2 * count : 3 * count]
    out = refs[-1]
    rows = jnp.concatenate([ref[...] for ref in mixed], axis=0)
    high, low = halves(rows)
    w_high = jnp.concatenate([ref[...] for ref in highs], axis=1)
    w_low = jnp.concatenate([ref[...] for ref in lows], axis=1)
    total = dot_split(w_high, w_low, high, low)
    if started:
        total = total + refs[3 * count][...]
    out[...] = total


def project(have, part, tables, peers, first, total):
    count = len(part)
    depth, length = have[0].shape
    high, low = tables
    width, columns = high.shape
    steps = columns // peers // depth
    whole = pl.BlockSpec((depth, length), lambda i: (0, 0))
    result = pl.BlockSpec((width, length), lambda i: (0, 0))

    def cut(o):
        return pl.BlockSpec((width, depth), lambda i: (0, o * steps + first))

    started = total is not None
    return call(
        functools.partial(project_body, count, started),
        jax.ShapeDtypeStruct((width, length), f32),
        grid_spec=pl.GridSpec(
            grid=(1,),
            in_specs=[whole] * count + [cut(o) for o in part] * 2 + [result] * started,
            out_specs=result,
        ),
        room=20,
        aliases={3 * count: 0} if started else None,
    )(*[have[o] for o in part], *[high] * count, *[low] * count, *([total] * started))


def swap(x, axis, size, offset):
    return lax.ppermute(x, axis, [(j, j ^ offset) for j in range(size)])


def gather(rows, peers, unit, tables, total, final):
    have = {0: rows}
    bit = peers // 2
    for o in range(1, bit):
        have[o] = swap(rows if o & (o - 1) == 0 else have[o & (o - 1)], "ch", peers, o & -o)
    far = swap(rows, "ch", peers, bit)
    if final:
        total = project(have, range(bit), tables, peers, unit, total)
        far, total = lax.optimization_barrier((far, total))
    have[bit] = far
    for o in range(1, bit):
        have[bit | o] = swap(far if o & (o - 1) == 0 else have[bit | (o & (o - 1))], "ch", peers, o & -o)
    if final:
        total = project(have, (bit,), tables, peers, unit, total)
        total = project(have, range(bit + 1, peers), tables, peers, unit, total)
    else:
        total = project(have, range(peers), tables, peers, unit, total)
    return total


def after(value, others):
    return lax.optimization_barrier((value, others))[0]


def per_device(query_rows, key_rows, value_rows, filters, skip_gain, out_weight):
    count = lax.axis_size("seq")
    peers = lax.axis_size("ch")
    length, channels = query_rows.shape
    slim = channels // count
    chunks = max(1, min(CHUNKS, slim // 8))
    group = LANES // slim
    width = out_weight.shape[1] // peers
    me = lax.axis_index("seq").astype(jnp.int32).reshape(1)
    mine = lax.axis_index("ch").astype(jnp.int32)
    forward, inverse = transforms(length)

    def pack_group(t, ready):
        pieces = pack(ready, key_rows, value_rows, filters, t, group, slim, chunks, 56 if t >= count // group // 2 else 8)
        for e in range(group):
            for k in range(chunks):
                sent[k][t * group + e] = pieces[e * chunks + k]
        return after(me, pieces)

    sent = [[None] * count for _ in range(chunks)]
    ready = me
    groups = count // group
    for t in list(range(groups // 2, groups)) + list(range(groups // 2)):
        ready = pack_group(t, ready)
    early, late = list(range(count // 2)), list(range(count // 2, count))
    arrived = [[None] * count for _ in range(chunks)]
    for k in range(chunks):
        for s in late + early:
            arrived[k][s] = swap(sent[k][s], "seq", count, s) if s else sent[k][0]
    blocks = cut(after(out_weight, ready), peers)
    blocks = lax.all_to_all(blocks, "ch", split_axis=0, concat_axis=0, tiled=True)
    gate, direct = gates(me, query_rows, key_rows, value_rows, skip_gain, count, chunks)

    total = None
    tables = None
    for k in range(chunks):
        near = spectrum([arrived[k][s] for s in early], forward)
        far = [arrived[k][s] for s in late]
        far, near, gate, direct = lax.optimization_barrier((far, near, gate, direct))
        back = [None] * count
        *pieces, left = convolve(me, early, late, near, far, forward, inverse)
        for s, piece in zip(late, pieces):
            back[s] = swap(piece, "seq", count, s)
        for s, piece in zip(early, restore(left, inverse, len(early))):
            back[s] = swap(piece, "seq", count, s) if s else piece
        if tables is None:
            tables = weights(after(me, left), mine.reshape(1), blocks, count, chunks)
        for u, unit in enumerate((early, late)):
            pieces = [back[s] for s in unit]
            if u:
                pieces, tables = lax.optimization_barrier((pieces, tables))
            rows = mix(pieces, gate, direct, k * count + unit[0])
            final = u and k == chunks - 1
            total = gather(rows, peers, k * 2 + u, tables, total, final)
    return total


def solution(mesh):
    in_specs = (
        P("seq", "ch"),
        P("seq", "ch"),
        P("seq", "ch"),
        P("seq", "ch"),
        P("ch"),
        P("ch", None),
    )
    out_specs = P("ch", "seq")
    return jax.shard_map(
        per_device, mesh=mesh, in_specs=in_specs, out_specs=out_specs, check_vma=False
    )
```

```python
import functools
import math

import jax
import jax.numpy as jnp
import ml_dtypes
import numpy as np
from jax import lax
from jax.experimental import pallas as pl
from jax.experimental.pallas import tpu as pltpu
from jax.sharding import PartitionSpec as P

LANES = 128
MIB = 1024 * 1024
CHUNKS = 1

f32 = jnp.float32
bf16 = jnp.bfloat16


def halves(x):
    high = x.astype(bf16)
    return high, (x - high.astype(f32)).astype(bf16)


def dot(a, b):
    return jnp.dot(a, b, preferred_element_type=f32)


def dot_split(a_high, a_low, b_high, b_low):
    return dot(a_high, b_high) + (dot(a_low, b_high) + dot(a_high, b_low))


def split_table(table):
    high = table.astype(np.float32).astype(ml_dtypes.bfloat16)
    low = (table - high.astype(np.float64)).astype(np.float32).astype(ml_dtypes.bfloat16)
    return jnp.asarray(high), jnp.asarray(low)


def transforms(length):
    orders = np.concatenate([np.arange(0, length, 2), np.arange(1, length, 2)])
    angle = math.pi / length * (orders[None, :] + 0.5) * np.arange(length)[:, None]
    forward = np.concatenate([np.cos(angle), -np.sin(angle)], axis=1)
    return split_table(forward), split_table(forward.T / length)


def near_core(x):
    return pltpu.with_memory_space_constraint(x, pltpu.VMEM)


def call(body, out_shape, *, grid_spec=None, in_specs=None, out_specs=None, scratch=(), room=16, aliases=None, work=1):
    params = pltpu.CompilerParams(vmem_limit_bytes=room * MIB)
    cost = pl.CostEstimate(flops=work, bytes_accessed=1, transcendentals=0)
    kwargs = dict(out_shape=out_shape, compiler_params=params, cost_estimate=cost)
    if aliases:
        kwargs["input_output_aliases"] = aliases
    if grid_spec is not None:
        return pl.pallas_call(body, grid_spec=grid_spec, **kwargs)
    return pl.pallas_call(body, in_specs=in_specs, out_specs=out_specs, scratch_shapes=list(scratch), **kwargs)


def pack_body(group, slim, chunks, order, me_ref, *rest):
    sources, rest = rest[:3], rest[3:]
    outs, (gated, taps), buffers, sems = rest[:-4], rest[-4:-2], rest[-2], rest[-1]
    part = slim // chunks
    me = me_ref[0]
    low = lax.rem(me, group)
    copies = {}
    for t in order:
        start = pl.multiple_of(jnp.bitwise_xor(me // group, t) * LANES, LANES)
        for a, source in enumerate(sources):
            copies[t, a] = pltpu.make_async_copy(source.at[:, pl.ds(start, LANES)], buffers.at[a, t], sems.at[a, t])
            copies[t, a].start()
    for t in order:
        for a in range(3):
            copies[t, a].wait()
        gated[...] = (buffers[0, t] * buffers[1, t]).T
        taps[...] = buffers[2, t].T
        for e in range(group):
            start = jnp.bitwise_xor(low, e) * slim
            for k in range(chunks):
                rows = pl.ds(pl.multiple_of(start + k * part, 8), part)
                out = outs[(t * group + e) * chunks + k]
                out[0:part, :] = gated[rows, :]
                out[part : 2 * part, :] = taps[rows, :]


def pack(me, key_rows, value_rows, filters, count, chunks):
    length, channels = key_rows.shape
    slim = channels // count
    group = LANES // slim
    steps = count // group
    order = list(range(steps // 2, steps)) + list(range(steps // 2))
    hbm = pl.BlockSpec(memory_space=pltpu.HBM)
    vmem = pl.BlockSpec(memory_space=pltpu.VMEM)
    return call(
        functools.partial(pack_body, group, slim, chunks, order),
        [jax.ShapeDtypeStruct((2 * slim // chunks, length), f32)] * (count * chunks),
        in_specs=[pl.BlockSpec(memory_space=pltpu.SMEM)] + [hbm] * 3,
        out_specs=[vmem] * (count * chunks),
        scratch=[
            pltpu.VMEM((LANES, length), f32),
            pltpu.VMEM((LANES, length), f32),
            pltpu.VMEM((3, steps, length, LANES), f32),
            pltpu.SemaphoreType.DMA((3, steps)),
        ],
        room=8,
    )(me, *(pltpu.with_memory_space_constraint(x, pltpu.HBM) for x in (key_rows, value_rows, filters)))


def spectrum_body(*refs):
    arrived, (fwd_high, fwd_low), out = refs[:-3], refs[-3:-1], refs[-1]
    rows = jnp.concatenate([ref[...] for ref in arrived], axis=0)
    high, low = halves(rows)
    out[...] = dot_split(high, low, fwd_high[...], fwd_low[...])


def spectrum(arrived, forward):
    double, length = arrived[0].shape
    vmem = pl.BlockSpec(memory_space=pltpu.VMEM)
    return call(
        spectrum_body,
        jax.ShapeDtypeStruct((len(arrived) * double, 2 * length), f32),
        in_specs=[vmem] * (2 + len(arrived)),
        out_specs=vmem,
        room=16,
    )(*arrived, *forward)


def products(count, part, length, spectra, totals):
    lane_steps = length // LANES

    def tile(index, carry):
        group = index // lane_steps
        lane = lax.rem(index, lane_steps)
        sign = jnp.where(lane * 2 < lane_steps, 1.0, -1.0).astype(f32)
        top = pl.ds(pl.multiple_of(group * 8, 8), 8)
        bottom = pl.ds(pl.multiple_of(part + group * 8, 8), 8)
        re = pl.ds(pl.multiple_of(lane * LANES, LANES), LANES)
        im = pl.ds(pl.multiple_of(length + lane * LANES, LANES), LANES)
        gated_re = [spectra[p, top, re] for p in range(count)]
        gated_im = [spectra[p, top, im] for p in range(count)]
        taps_re, taps_im = [], []
        last_re = last_im = None
        for q in range(count):
            now_re, now_im = spectra[q, bottom, re], spectra[q, bottom, im]
            if q == 0:
                taps_re.append(now_re)
                taps_im.append(now_im)
            else:
                taps_re.append(now_re - sign * last_im)
                taps_im.append(now_im + sign * last_re)
            last_re, last_im = now_re, now_im
        for i in range(count):
            total_re = total_im = None
            for p in range(i + 1):
                a_re, a_im = gated_re[p], gated_im[p]
                b_re, b_im = taps_re[i - p], taps_im[i - p]
                one_re = a_re * b_re - a_im * b_im
                one_im = a_re * b_im + a_im * b_re
                total_re = one_re if p == 0 else total_re + one_re
                total_im = one_im if p == 0 else total_im + one_im
            totals[i, top, re] = total_re
            totals[i, top, im] = total_im
        return carry

    lax.fori_loop(0, part // 8 * lane_steps, tile, 0)


def conv_body(early, late, far, me_ref, fwd_high, fwd_low, inv_high, inv_low, *rest):
    arrived, rest = rest[: len(late)], rest[len(late) :]
    known, rest = rest[: len(early)], rest[len(early) :]
    outs, (left, spectra, totals) = rest[: len(far)], rest[len(far) :]
    count = sum(map(len, early)) + len(late)
    near = [s for s in range(count) if s not in far]
    me = me_ref[0]
    double, length = arrived[0].shape
    part = double // 2
    for group, one in zip(early, known):
        for e, s in enumerate(group):
            spectra[jnp.bitwise_xor(me, s)] = one[e * double : (e + 1) * double, :]
    rows = jnp.concatenate([ref[...] for ref in arrived], axis=0)
    high, low = halves(rows)
    result = dot_split(high, low, fwd_high[...], fwd_low[...])
    for e, s in enumerate(late):
        spectra[jnp.bitwise_xor(me, s)] = result[e * double : (e + 1) * double]
    products(count, part, length, spectra, totals)
    stacked = jnp.concatenate([totals[jnp.bitwise_xor(me, s)] for s in far], axis=0)
    high, low = halves(stacked)
    result = dot_split(high, low, inv_high[...], inv_low[...])
    for e in range(len(far)):
        outs[e][...] = result[e * part : (e + 1) * part]
    for e, s in enumerate(near):
        left[e * part : (e + 1) * part, :] = totals[jnp.bitwise_xor(me, s)]


def convolve(me, early, late, far, known, arrived, forward, inverse):
    count = sum(map(len, early)) + len(late)
    double, length = arrived[0].shape
    part = double // 2
    vmem = pl.BlockSpec(memory_space=pltpu.VMEM)
    return call(
        functools.partial(conv_body, early, late, far),
        [jax.ShapeDtypeStruct((part, length), f32)] * len(far)
        + [jax.ShapeDtypeStruct(((count - len(far)) * part, 2 * length), f32)],
        in_specs=[pl.BlockSpec(memory_space=pltpu.SMEM)] + [vmem] * (4 + len(late) + len(early)),
        out_specs=[vmem] * (len(far) + 1),
        scratch=[
            pltpu.VMEM((count, double, 2 * length), f32),
            pltpu.VMEM((count, part, 2 * length), f32),
        ],
        room=24,
    )(me, *forward, *inverse, *arrived, *known)


def restore_body(left, inv_high, inv_low, *outs):
    part = outs[0].shape[0]
    high, low = halves(left[...])
    result = dot_split(high, low, inv_high[...], inv_low[...])
    for e, out in enumerate(outs):
        out[...] = result[e * part : (e + 1) * part]


def restore(left, inverse, pieces):
    rows, width = left.shape
    vmem = pl.BlockSpec(memory_space=pltpu.VMEM)
    return call(
        restore_body,
        [jax.ShapeDtypeStruct((rows // pieces, width // 2), f32)] * pieces,
        in_specs=[vmem] * 3,
        out_specs=[vmem] * pieces,
        room=16,
    )(left, *inverse)


def gates_body(count, chunks, me_ref, query_ref, key_ref, value_ref, skip_ref, gate_ref, direct_ref, gate_t, direct_t):
    query = query_ref[...]
    gate_t[...] = query.T
    direct_t[...] = (query * (skip_ref[...] * (key_ref[...] * value_ref[...]))).T
    slim = gate_t.shape[0] // count
    part = slim // chunks
    for k in range(chunks):
        for s in range(count):
            start = jnp.bitwise_xor(me_ref[0], s) * slim + k * part
            source = pl.ds(pl.multiple_of(start, 8), part)
            here = pl.ds((k * count + s) * part, part)
            gate_ref[here, :] = gate_t[source, :]
            direct_ref[here, :] = direct_t[source, :]


def gates(me, query_rows, key_rows, value_rows, skip_gain, count, chunks):
    length, channels = query_rows.shape
    vmem = pl.BlockSpec(memory_space=pltpu.VMEM)
    return call(
        functools.partial(gates_body, count, chunks),
        [jax.ShapeDtypeStruct((channels, length), f32)] * 2,
        in_specs=[pl.BlockSpec(memory_space=pltpu.SMEM)] + [vmem] * 4,
        out_specs=[vmem] * 2,
        scratch=[pltpu.VMEM((channels, length), f32)] * 2,
        room=16,
        work=8 * 10**10,
    )(me, query_rows, key_rows, value_rows, skip_gain[None, :])


def mix_body(first, chained, *refs):
    out, whole = refs[-2:]
    *pieces, gate, direct = refs[: len(refs) - 2 - chained]
    part = pieces[0].shape[0]
    for e, piece in enumerate(pieces):
        rows = pl.ds((first + e) * part, part)
        mixed = gate[rows, :] * piece[...] + direct[rows, :]
        out[e * part : (e + 1) * part, :] = mixed
        whole[rows, :] = mixed


def mix(pieces, gate, direct, first, whole):
    part, length = pieces[0].shape
    count = len(pieces)
    vmem = pl.BlockSpec(memory_space=pltpu.VMEM)
    chained = [] if whole is None else [whole]
    return call(
        functools.partial(mix_body, first, len(chained)),
        [jax.ShapeDtypeStruct((count * part, length), f32), jax.ShapeDtypeStruct(gate.shape, f32)],
        in_specs=[vmem] * (count + 2 + len(chained)),
        out_specs=[vmem] * 2,
        room=8,
        aliases={count + 2: 1} if chained else None,
    )(*pieces, gate, direct, *chained)


def cut_body(weight_ref, out_ref):
    out_ref[0] = weight_ref[...]


def cut(out_weight, peers):
    channels, total = out_weight.shape
    width = total // peers
    return call(
        cut_body,
        jax.ShapeDtypeStruct((peers, channels, width), f32),
        grid_spec=pl.GridSpec(
            grid=(peers,),
            in_specs=[pl.BlockSpec((channels, width), lambda o: (0, o))],
            out_specs=pl.BlockSpec((1, channels, width), lambda o: (o, 0, 0)),
        ),
        room=8,
    )(pltpu.with_memory_space_constraint(out_weight, pltpu.HBM))


def weights_body(count, chunks, me_ref, mine_ref, weight_ref, high_ref, low_ref, ordered):
    slim = ordered.shape[0] // count
    part = slim // chunks
    for k in range(chunks):
        for s in range(count):
            start = jnp.bitwise_xor(me_ref[0], s) * slim + k * part
            ordered[pl.ds((k * count + s) * part, part), :] = weight_ref[0, pl.ds(pl.multiple_of(start, 8), part), :]
    high, low = halves(ordered[...].T)
    high_ref[...] = high
    low_ref[...] = low


def weights(me, mine, blocks, count, chunks):
    peers, channels, width = blocks.shape
    result = pl.BlockSpec((width, channels), lambda o, me_ref, mine_ref: (0, o))
    return call(
        functools.partial(weights_body, count, chunks),
        [jax.ShapeDtypeStruct((width, peers * channels), bf16)] * 2,
        grid_spec=pltpu.PrefetchScalarGridSpec(
            num_scalar_prefetch=2,
            grid=(peers,),
            in_specs=[pl.BlockSpec((1, channels, width), lambda o, me_ref, mine_ref: (jnp.bitwise_xor(mine_ref[0], o), 0, 0))],
            out_specs=[result] * 2,
            scratch_shapes=[pltpu.VMEM((channels, width), f32)],
        ),
        room=12,
        work=3 * 10**10,
    )(me, mine, blocks)


def project_body(entries, started, final, *refs):
    count = 1 + max(entry[0] for entry in entries)
    before, refs = refs[:started], refs[started:]
    mixed, (table_high, table_low), rest = refs[:count], refs[count : count + 2], refs[count + 2 :]
    rows = jnp.concatenate([mixed[i][a : a + n, :] for i, a, n, _ in entries], axis=0)
    high, low = halves(rows)
    out = rest[0]
    steps = 4 if final else 1
    span = out.shape[0] // steps
    copies = []
    for r in range(steps):
        here = pl.ds(r * span, span)
        w_high = jnp.concatenate([table_high[here, c : c + n] for _, _, n, c in entries], axis=1)
        w_low = jnp.concatenate([table_low[here, c : c + n] for _, _, n, c in entries], axis=1)
        total = dot_split(w_high, w_low, high, low)
        if started:
            total = total + before[0][here, :]
        if final:
            held, sems = rest[-2:]
            held[here, :] = total
            copies.append(pltpu.make_async_copy(held.at[here, :], out.at[here, :], sems.at[r]))
            copies[-1].start()
        else:
            out[...] = total
    for copy in copies:
        copy.wait()


def project(entries, tables, total=None, final=False, work=1):
    arrays, places = [], []
    for array, *place in entries:
        found = [i for i, other in enumerate(arrays) if other is array]
        if not found:
            arrays.append(array)
        places.append((found[0] if found else len(arrays) - 1, *place))
    length = arrays[0].shape[1]
    high, low = tables
    width = high.shape[0]
    vmem = pl.BlockSpec(memory_space=pltpu.VMEM)
    started = total is not None
    return call(
        functools.partial(project_body, places, started, final),
        jax.ShapeDtypeStruct((width, length), f32),
        in_specs=[vmem] * (len(arrays) + 2 + started),
        out_specs=pl.BlockSpec(memory_space=pltpu.HBM) if final else vmem,
        scratch=[pltpu.VMEM((width, length), f32), pltpu.SemaphoreType.DMA((4,))] if final else [],
        room=16,
        work=work,
    )(*([total] * started), *map(near_core, arrays), high, low)


def swap(x, axis, size, offset):
    return lax.ppermute(x, axis, [(j, j ^ offset) for j in range(size)])


def spread(x, bit):
    found = {0: x}
    for o in range(1, bit):
        found[o] = swap(found[o & (o - 1)], "ch", lax.axis_size("ch"), o & -o)
    return found


def after(value, others):
    return lax.optimization_barrier((value, others))[0]


def per_device(query_rows, key_rows, value_rows, filters, skip_gain, out_weight):
    count = lax.axis_size("seq")
    peers = lax.axis_size("ch")
    length, channels = query_rows.shape
    slim = channels // count
    chunks = max(1, min(CHUNKS, slim // 8))
    width = out_weight.shape[1] // peers
    me = lax.axis_index("seq").astype(jnp.int32).reshape(1)
    mine = lax.axis_index("ch").astype(jnp.int32)
    forward, inverse = transforms(length)

    pieces = pack(me, key_rows, value_rows, filters, count, chunks)
    sent = [pieces[k::chunks] for k in range(chunks)]
    half = count // 2
    near, far = list(range(half)), list(range(half, count))
    arrived = [[None] * count for _ in range(chunks)]
    for k in range(chunks):
        for s in far:
            arrived[k][s] = swap(sent[k][s], "seq", count, s)
        for s in near[1:]:
            piece = sent[k][s] if s < 3 else after(sent[k][s], arrived[k][s - 1])
            arrived[k][s] = swap(piece, "seq", count, s)
        arrived[k][0] = sent[k][0]
    blocks = cut(after(out_weight, sent[0][half]), peers)
    blocks = lax.all_to_all(blocks, "ch", split_axis=0, concat_axis=0, tiled=True)

    gate, direct = gates(me, query_rows, key_rows, value_rows, skip_gain, count, chunks)
    early, late = [near], far
    part = slim // chunks
    units = [near, far]
    if half // 2 * part % LANES == 0:
        units = [near, far[: half // 2], far[half // 2 :]]
    total = None
    tables = None
    for k in range(chunks):
        known = [spectrum([arrived[k][s] for s in group], forward) for group in early]
        last = [arrived[k][s] for s in late]
        last, known, gate, direct = lax.optimization_barrier((last, known, gate, direct))
        back = [None] * count
        *pieces, left = convolve(me, early, late, far, known, last, forward, inverse)
        for s, piece in zip(far, pieces):
            back[s] = swap(piece, "seq", count, s)
        for s, piece in zip(near, restore(left, inverse, half)):
            back[s] = swap(piece, "seq", count, s) if s else piece
        if tables is None:
            tables = weights(after(me, left), mine.reshape(1), blocks, count, chunks)
        bit = peers // 2
        own, far_own, whole = [], [], None
        last = len(units) - 1
        starts = [unit[0] * part for unit in units]
        sizes = [len(unit) * part for unit in units]

        def entry(array, u, o, row=0):
            return (array, row, sizes[u], o * channels + starts[u])

        for u, unit in enumerate(units):
            pieces = [back[s] for s in unit]
            if u:
                total = project([entry(own[u - 1], u - 1, 0)], tables, total, work=3 * 10**10)
                total, pieces = lax.optimization_barrier((total, pieces))
            alone, whole = mix(pieces, gate, direct, unit[0], whole)
            own.append(alone)
            far_own.append(swap(alone, "ch", peers, bit))

    beside = spread(whole, bit)
    across = [spread(after(x, own[last]), bit) for x in far_own[:last]]
    total = project([entry(own[last], last, 0), entry(across[0][0], 0, bit)], tables, total, work=3 * 10**10)
    total = project([(beside[o], 0, channels, o * channels) for o in range(1, bit)], tables, total, work=3 * 10**10)
    if last > 1:
        entries = [entry(across[u][0], u, bit) for u in range(1, last)]
        entries += [entry(across[u][o], u, bit | o) for u in range(last - 1) for o in range(1, bit)]
        total = project(entries, tables, total, work=3 * 10**10)
    total, ending = lax.optimization_barrier((total, far_own[last]))
    ending = spread(ending, bit)
    entries = [entry(ending[0], last, bit)]
    entries += [entry(across[last - 1][o], last - 1, bit | o) for o in range(1, bit)]
    total = project(entries, tables, total)
    total = project([entry(ending[o], last, bit | o) for o in range(1, bit)], tables, total, True)
    return total


def solution(mesh):
    in_specs = (
        P("seq", "ch"),
        P("seq", "ch"),
        P("seq", "ch"),
        P("seq", "ch"),
        P("ch"),
        P("ch", None),
    )
    out_specs = P("ch", "seq")
    return jax.shard_map(
        per_device, mesh=mesh, in_specs=in_specs, out_specs=out_specs, check_vma=False
    )
```

```python
import functools
import math

import jax
import jax.numpy as jnp
import ml_dtypes
import numpy as np
from jax import lax
from jax.experimental import pallas as pl
from jax.experimental.pallas import tpu as pltpu
from jax.sharding import PartitionSpec as P

LANES = 128
MIB = 1024 * 1024
CHUNKS = 1

f32 = jnp.float32
bf16 = jnp.bfloat16


def halves(x):
    high = x.astype(bf16)
    return high, (x - high.astype(f32)).astype(bf16)


def dot(a, b):
    return jnp.dot(a, b, preferred_element_type=f32)


def dot_split(a_high, a_low, b_high, b_low):
    return dot(a_high, b_high) + (dot(a_low, b_high) + dot(a_high, b_low))


def split_table(table):
    high = table.astype(np.float32).astype(ml_dtypes.bfloat16)
    low = (table - high.astype(np.float64)).astype(np.float32).astype(ml_dtypes.bfloat16)
    return jnp.asarray(high), jnp.asarray(low)


def transforms(length):
    orders = np.concatenate([np.arange(0, length, 2), np.arange(1, length, 2)])
    angle = math.pi / length * (orders[None, :] + 0.5) * np.arange(length)[:, None]
    forward = np.concatenate([np.cos(angle), -np.sin(angle)], axis=1)
    return split_table(forward), split_table(forward.T / length)


def near_core(x):
    return pltpu.with_memory_space_constraint(x, pltpu.VMEM)


def call(body, out_shape, *, grid_spec=None, in_specs=None, out_specs=None, scratch=(), room=16, aliases=None, work=1):
    params = pltpu.CompilerParams(vmem_limit_bytes=room * MIB)
    cost = pl.CostEstimate(flops=work, bytes_accessed=1, transcendentals=0)
    kwargs = dict(out_shape=out_shape, compiler_params=params, cost_estimate=cost)
    if aliases:
        kwargs["input_output_aliases"] = aliases
    if grid_spec is not None:
        return pl.pallas_call(body, grid_spec=grid_spec, **kwargs)
    return pl.pallas_call(body, in_specs=in_specs, out_specs=out_specs, scratch_shapes=list(scratch), **kwargs)


def pack_body(group, slim, chunks, order, me_ref, *rest):
    sources, rest = rest[:3], rest[3:]
    outs, (gated, taps), buffers, sems = rest[:-4], rest[-4:-2], rest[-2], rest[-1]
    part = slim // chunks
    me = me_ref[0]
    low = lax.rem(me, group)
    copies = {}
    for t in order:
        start = pl.multiple_of(jnp.bitwise_xor(me // group, t) * LANES, LANES)
        for a, source in enumerate(sources):
            copies[t, a] = pltpu.make_async_copy(source.at[:, pl.ds(start, LANES)], buffers.at[a, t], sems.at[a, t])
            copies[t, a].start()
    for t in order:
        for a in range(3):
            copies[t, a].wait()
        gated[...] = (buffers[0, t] * buffers[1, t]).T
        taps[...] = buffers[2, t].T
        for e in range(group):
            start = jnp.bitwise_xor(low, e) * slim
            for k in range(chunks):
                rows = pl.ds(pl.multiple_of(start + k * part, 8), part)
                out = outs[(t * group + e) * chunks + k]
                out[0:part, :] = gated[rows, :]
                out[part : 2 * part, :] = taps[rows, :]


def pack(me, key_rows, value_rows, filters, count, chunks):
    length, channels = key_rows.shape
    slim = channels // count
    group = LANES // slim
    steps = count // group
    order = list(range(steps // 2, steps)) + list(range(steps // 2))
    hbm = pl.BlockSpec(memory_space=pltpu.HBM)
    vmem = pl.BlockSpec(memory_space=pltpu.VMEM)
    return call(
        functools.partial(pack_body, group, slim, chunks, order),
        [jax.ShapeDtypeStruct((2 * slim // chunks, length), f32)] * (count * chunks),
        in_specs=[pl.BlockSpec(memory_space=pltpu.SMEM)] + [hbm] * 3,
        out_specs=[vmem] * (count * chunks),
        scratch=[
            pltpu.VMEM((LANES, length), f32),
            pltpu.VMEM((LANES, length), f32),
            pltpu.VMEM((3, steps, length, LANES), f32),
            pltpu.SemaphoreType.DMA((3, steps)),
        ],
        room=8,
    )(me, *(pltpu.with_memory_space_constraint(x, pltpu.HBM) for x in (key_rows, value_rows, filters)))


def spectrum_body(slots, chained, me_ref, fwd_high, fwd_low, *refs):
    arrived, out = refs[: len(slots)], refs[-1]
    double = arrived[0].shape[0]
    rows = jnp.concatenate([ref[...] for ref in arrived], axis=0)
    high, low = halves(rows)
    result = dot_split(high, low, fwd_high[...], fwd_low[...])
    for e, s in enumerate(slots):
        out[jnp.bitwise_xor(me_ref[0], s)] = result[e * double : (e + 1) * double]


def spectrum(me, slots, arrived, forward, count, spectra):
    double, length = arrived[0].shape
    vmem = pl.BlockSpec(memory_space=pltpu.VMEM)
    chained = [] if spectra is None else [spectra]
    return call(
        functools.partial(spectrum_body, slots, len(chained)),
        jax.ShapeDtypeStruct((count, double, 2 * length), f32),
        in_specs=[pl.BlockSpec(memory_space=pltpu.SMEM)] + [vmem] * (2 + len(arrived) + len(chained)),
        out_specs=vmem,
        room=16,
        aliases={3 + len(arrived): 0} if chained else None,
    )(me, *forward, *arrived, *chained)


def products(count, part, length, spectra, totals):
    lane_steps = length // LANES

    def tile(index, carry):
        group = index // lane_steps
        lane = lax.rem(index, lane_steps)
        sign = jnp.where(lane * 2 < lane_steps, 1.0, -1.0).astype(f32)
        top = pl.ds(pl.multiple_of(group * 8, 8), 8)
        bottom = pl.ds(pl.multiple_of(part + group * 8, 8), 8)
        re = pl.ds(pl.multiple_of(lane * LANES, LANES), LANES)
        im = pl.ds(pl.multiple_of(length + lane * LANES, LANES), LANES)
        gated_re = [spectra[p, top, re] for p in range(count)]
        gated_im = [spectra[p, top, im] for p in range(count)]
        taps_re, taps_im = [], []
        last_re = last_im = None
        for q in range(count):
            now_re, now_im = spectra[q, bottom, re], spectra[q, bottom, im]
            if q == 0:
                taps_re.append(now_re)
                taps_im.append(now_im)
            else:
                taps_re.append(now_re - sign * last_im)
                taps_im.append(now_im + sign * last_re)
            last_re, last_im = now_re, now_im
        gated_sum = [a + b for a, b in zip(gated_re, gated_im)]
        taps_sum = [a + b for a, b in zip(taps_re, taps_im)]
        for i in range(count):
            reals, imags, sums = (
                sum(a[p] * b[i - p] for p in range(1, i + 1)) + a[0] * b[i]
                for a, b in ((gated_re, taps_re), (gated_im, taps_im), (gated_sum, taps_sum))
            )
            totals[i, top, re] = reals - imags
            totals[i, top, im] = sums - reals - imags
        return carry

    lax.fori_loop(0, part // 8 * lane_steps, tile, 0)


def conv_body(late, far, count, me_ref, fwd_high, fwd_low, inv_high, inv_low, *rest):
    arrived, rest = rest[: len(late)], rest[len(late) + 1 :]
    outs, (left, spectra, totals) = rest[: len(far)], rest[len(far) :]
    near = [s for s in range(count) if s not in far]
    me = me_ref[0]
    double, length = arrived[0].shape
    part = double // 2
    rows = jnp.concatenate([ref[...] for ref in arrived], axis=0)
    high, low = halves(rows)
    result = dot_split(high, low, fwd_high[...], fwd_low[...])
    for e, s in enumerate(late):
        spectra[jnp.bitwise_xor(me, s)] = result[e * double : (e + 1) * double]
    products(count, part, length, spectra, totals)
    stacked = jnp.concatenate([totals[jnp.bitwise_xor(me, s)] for s in far], axis=0)
    high, low = halves(stacked)
    result = dot_split(high, low, inv_high[...], inv_low[...])
    for e in range(len(far)):
        outs[e][...] = result[e * part : (e + 1) * part]
    for e, s in enumerate(near):
        left[e * part : (e + 1) * part, :] = totals[jnp.bitwise_xor(me, s)]


def convolve(me, late, far, arrived, spectra, forward, inverse):
    count = spectra.shape[0]
    double, length = arrived[0].shape
    part = double // 2
    vmem = pl.BlockSpec(memory_space=pltpu.VMEM)
    *pieces, left, _ = call(
        functools.partial(conv_body, late, far, count),
        [jax.ShapeDtypeStruct((part, length), f32)] * len(far)
        + [
            jax.ShapeDtypeStruct(((count - len(far)) * part, 2 * length), f32),
            jax.ShapeDtypeStruct(spectra.shape, f32),
        ],
        in_specs=[pl.BlockSpec(memory_space=pltpu.SMEM)] + [vmem] * (5 + len(late)),
        out_specs=[vmem] * (len(far) + 2),
        scratch=[pltpu.VMEM((count, part, 2 * length), f32)],
        room=24,
        aliases={5 + len(late): len(far) + 1},
    )(me, *forward, *inverse, *arrived, spectra)
    return pieces, left


def restore_body(left, inv_high, inv_low, *outs):
    part = outs[0].shape[0]
    high, low = halves(left[...])
    result = dot_split(high, low, inv_high[...], inv_low[...])
    for e, out in enumerate(outs):
        out[...] = result[e * part : (e + 1) * part]


def restore(left, inverse, pieces):
    rows, width = left.shape
    vmem = pl.BlockSpec(memory_space=pltpu.VMEM)
    return call(
        restore_body,
        [jax.ShapeDtypeStruct((rows // pieces, width // 2), f32)] * pieces,
        in_specs=[vmem] * 3,
        out_specs=[vmem] * pieces,
        room=16,
    )(left, *inverse)


def gates_body(count, units, me_ref, query_ref, key_ref, value_ref, skip_ref, *refs):
    outs, (gate_t, direct_t) = refs[:-2], refs[-2:]
    query = query_ref[...]
    gate_t[...] = query.T
    direct_t[...] = (query * (skip_ref[...] * (key_ref[...] * value_ref[...]))).T
    part = gate_t.shape[0] // count
    for u, unit in enumerate(units):
        for e, s in enumerate(unit):
            source = pl.ds(pl.multiple_of(jnp.bitwise_xor(me_ref[0], s) * part, 8), part)
            here = pl.ds(e * part, part)
            outs[2 * u][here, :] = gate_t[source, :]
            outs[2 * u + 1][here, :] = direct_t[source, :]


def gates(me, query_rows, key_rows, value_rows, skip_gain, count, units):
    length, channels = query_rows.shape
    part = channels // count
    vmem = pl.BlockSpec(memory_space=pltpu.VMEM)
    flat = call(
        functools.partial(gates_body, count, units),
        [jax.ShapeDtypeStruct((len(unit) * part, length), f32) for unit in units for _ in range(2)],
        in_specs=[pl.BlockSpec(memory_space=pltpu.SMEM)] + [vmem] * 4,
        out_specs=[vmem] * (2 * len(units)),
        scratch=[pltpu.VMEM((channels, length), f32)] * 2,
        room=16,
        work=80 * 10**9,
    )(me, query_rows, key_rows, value_rows, skip_gain[None, :])
    return [flat[2 * u : 2 * u + 2] for u in range(len(units))]


def mix_body(first, chained, *refs):
    out, whole = refs[-2:]
    *pieces, gate, direct = refs[: len(refs) - 2 - chained]
    part = pieces[0].shape[0]
    for e, piece in enumerate(pieces):
        here = pl.ds(e * part, part)
        mixed = gate[here, :] * piece[...] + direct[here, :]
        out[here, :] = mixed
        whole[pl.ds((first + e) * part, part), :] = mixed


def mix(pieces, gate, direct, first, count, whole):
    part, length = pieces[0].shape
    held = len(pieces)
    vmem = pl.BlockSpec(memory_space=pltpu.VMEM)
    chained = [] if whole is None else [whole]
    return call(
        functools.partial(mix_body, first, len(chained)),
        [jax.ShapeDtypeStruct((held * part, length), f32), jax.ShapeDtypeStruct((count * part, length), f32)],
        in_specs=[vmem] * (held + 2 + len(chained)),
        out_specs=[vmem] * 2,
        room=8,
        aliases={held + 2: 1} if chained else None,
    )(*pieces, gate, direct, *chained)


def cut_body(weight_ref, out_ref):
    out_ref[0] = weight_ref[...]


def cut(out_weight, peers):
    channels, total = out_weight.shape
    width = total // peers
    return call(
        cut_body,
        jax.ShapeDtypeStruct((peers, channels, width), f32),
        grid_spec=pl.GridSpec(
            grid=(peers,),
            in_specs=[pl.BlockSpec((channels, width), lambda o: (0, o))],
            out_specs=pl.BlockSpec((1, channels, width), lambda o: (o, 0, 0)),
        ),
        room=8,
    )(pltpu.with_memory_space_constraint(out_weight, pltpu.HBM))


def weights_body(count, chunks, me_ref, mine_ref, weight_ref, high_ref, low_ref, ordered):
    slim = ordered.shape[0] // count
    part = slim // chunks
    for k in range(chunks):
        for s in range(count):
            start = jnp.bitwise_xor(me_ref[0], s) * slim + k * part
            ordered[pl.ds((k * count + s) * part, part), :] = weight_ref[0, pl.ds(pl.multiple_of(start, 8), part), :]
    high, low = halves(ordered[...].T)
    high_ref[...] = high
    low_ref[...] = low


def weights(me, mine, blocks, count, chunks):
    peers, channels, width = blocks.shape
    result = pl.BlockSpec((width, channels), lambda o, me_ref, mine_ref: (0, o))
    return call(
        functools.partial(weights_body, count, chunks),
        [jax.ShapeDtypeStruct((width, peers * channels), bf16)] * 2,
        grid_spec=pltpu.PrefetchScalarGridSpec(
            num_scalar_prefetch=2,
            grid=(peers,),
            in_specs=[pl.BlockSpec((1, channels, width), lambda o, me_ref, mine_ref: (jnp.bitwise_xor(mine_ref[0], o), 0, 0))],
            out_specs=[result] * 2,
            scratch_shapes=[pltpu.VMEM((channels, width), f32)],
        ),
        room=12,
        work=20 * 10**9,
    )(me, mine, blocks)


def project_body(entries, started, final, *refs):
    count = 1 + max(entry[0] for entry in entries)
    before, refs = refs[:started], refs[started:]
    mixed, (table_high, table_low), rest = refs[:count], refs[count : count + 2], refs[count + 2 :]
    rows = jnp.concatenate([mixed[i][a : a + n, :] for i, a, n, _ in entries], axis=0)
    high, low = halves(rows)
    out = rest[0]
    steps = 4 if final else 1
    span = out.shape[0] // steps
    copies = []
    for r in range(steps):
        here = pl.ds(r * span, span)
        w_high = jnp.concatenate([table_high[here, c : c + n] for _, _, n, c in entries], axis=1)
        w_low = jnp.concatenate([table_low[here, c : c + n] for _, _, n, c in entries], axis=1)
        total = dot_split(w_high, w_low, high, low)
        if started:
            total = total + before[0][here, :]
        if final:
            held, sems = rest[-2:]
            held[here, :] = total
            copies.append(pltpu.make_async_copy(held.at[here, :], out.at[here, :], sems.at[r]))
            copies[-1].start()
        else:
            out[...] = total
    for copy in copies:
        copy.wait()


def project(entries, tables, total=None, final=False, work=1):
    arrays, places = [], []
    for array, *place in entries:
        found = [i for i, other in enumerate(arrays) if other is array]
        if not found:
            arrays.append(array)
        places.append((found[0] if found else len(arrays) - 1, *place))
    length = arrays[0].shape[1]
    high, low = tables
    width = high.shape[0]
    vmem = pl.BlockSpec(memory_space=pltpu.VMEM)
    started = total is not None
    return call(
        functools.partial(project_body, places, started, final),
        jax.ShapeDtypeStruct((width, length), f32),
        in_specs=[vmem] * (len(arrays) + 2 + started),
        out_specs=pl.BlockSpec(memory_space=pltpu.HBM) if final else vmem,
        scratch=[pltpu.VMEM((width, length), f32), pltpu.SemaphoreType.DMA((4,))] if final else [],
        room=16,
        work=work,
    )(*([total] * started), *map(near_core, arrays), high, low)


def swap(x, axis, size, offset):
    return lax.ppermute(x, axis, [(j, j ^ offset) for j in range(size)])


def spread(x, bit):
    found = {0: x}
    for o in range(1, bit):
        found[o] = swap(found[o & (o - 1)], "ch", lax.axis_size("ch"), o & -o)
    return found


def after(value, others):
    return lax.optimization_barrier((value, others))[0]


def per_device(query_rows, key_rows, value_rows, filters, skip_gain, out_weight):
    count = lax.axis_size("seq")
    peers = lax.axis_size("ch")
    length, channels = query_rows.shape
    slim = channels // count
    chunks = max(1, min(CHUNKS, slim // 8))
    width = out_weight.shape[1] // peers
    me = lax.axis_index("seq").astype(jnp.int32).reshape(1)
    mine = lax.axis_index("ch").astype(jnp.int32)
    forward, inverse = transforms(length)

    pieces = pack(me, key_rows, value_rows, filters, count, chunks)
    sent = [pieces[k::chunks] for k in range(chunks)]
    half = count // 2
    near, far = list(range(half)), list(range(half, count))
    arrived = [[None] * count for _ in range(chunks)]
    for k in range(chunks):
        for s in far:
            arrived[k][s] = swap(sent[k][s], "seq", count, s)
        for s in near[1:]:
            piece = sent[k][s] if s < 3 else after(sent[k][s], arrived[k][s - 1])
            arrived[k][s] = swap(piece, "seq", count, s)
        arrived[k][0] = sent[k][0]
    blocks = cut(after(out_weight, sent[0][half]), peers)
    blocks = lax.all_to_all(blocks, "ch", split_axis=0, concat_axis=0, tiled=True)

    part = slim // chunks
    units = [near, far]
    if half // 2 * part % LANES == 0:
        units = [near, far[: half // 2], far[half // 2 :]]
    gated = gates(me, query_rows, key_rows, value_rows, skip_gain, count, units)
    early, late = [near, far[: half // 2]], far[half // 2 :]
    total = None
    tables = None
    for k in range(chunks):
        spectra = None
        for slots in early:
            pieces = [arrived[k][s] for s in slots]
            if spectra is not None:
                spectra, pieces = lax.optimization_barrier((spectra, pieces))
            spectra = spectrum(me, slots, pieces, forward, count, spectra)
        last = [arrived[k][s] for s in late]
        spectra, last, gated = lax.optimization_barrier((spectra, last, gated))
        back = [None] * count
        pieces, left = convolve(me, late, far, last, spectra, forward, inverse)
        for s, piece in zip(far, pieces):
            back[s] = swap(piece, "seq", count, s)
        for s, piece in zip(near, restore(left, inverse, half)):
            back[s] = swap(piece, "seq", count, s) if s else piece
        if tables is None:
            tables = weights(after(me, left), mine.reshape(1), blocks, count, chunks)
        bit = peers // 2
        own, far_own, whole = [], [], None
        last = len(units) - 1
        starts = [unit[0] * part for unit in units]
        sizes = [len(unit) * part for unit in units]

        def entry(array, u, o, row=0):
            return (array, row, sizes[u], o * channels + starts[u])

        for u, unit in enumerate(units):
            pieces = [back[s] for s in unit]
            if u:
                total = project([entry(own[u - 1], u - 1, 0)], tables, total, work=20 * 10**9)
                total, pieces = lax.optimization_barrier((total, pieces))
            alone, whole = mix(pieces, *gated[u], unit[0], count, whole)
            own.append(alone)
            far_own.append(swap(alone, "ch", peers, bit))

    beside = spread(whole, bit)
    across = [spread(after(x, own[last]), bit) for x in far_own[:last]]
    total = project([entry(own[last], last, 0), entry(across[0][0], 0, bit)], tables, total, work=20 * 10**9)
    total = project([(beside[o], 0, channels, o * channels) for o in range(1, bit)], tables, total, work=20 * 10**9)
    if last > 1:
        entries = [entry(across[u][0], u, bit) for u in range(1, last)]
        entries += [entry(across[u][o], u, bit | o) for u in range(last - 1) for o in range(1, bit)]
        total = project(entries, tables, total, work=20 * 10**9)
    total, ending = lax.optimization_barrier((total, far_own[last]))
    ending = spread(ending, bit)
    entries = [entry(ending[0], last, bit)]
    entries += [entry(across[last - 1][o], last - 1, bit | o) for o in range(1, bit)]
    total = project(entries, tables, total)
    total = project([entry(ending[o], last, bit | o) for o in range(1, bit)], tables, total, True)
    return total


def solution(mesh):
    in_specs = (
        P("seq", "ch"),
        P("seq", "ch"),
        P("seq", "ch"),
        P("seq", "ch"),
        P("ch"),
        P("ch", None),
    )
    out_specs = P("ch", "seq")
    return jax.shard_map(
        per_device, mesh=mesh, in_specs=in_specs, out_specs=out_specs, check_vma=False
    )
```

```python
import functools
import math

import jax
import jax.numpy as jnp
import ml_dtypes
import numpy as np
from jax import lax
from jax.experimental import pallas as pl
from jax.experimental.pallas import tpu as pltpu
from jax.sharding import PartitionSpec as P

LANES = 128
MIB = 1024 * 1024
CHUNKS = 1

f32 = jnp.float32
bf16 = jnp.bfloat16


def halves(x):
    high = x.astype(bf16)
    return high, (x - high.astype(f32)).astype(bf16)


def dot(a, b):
    return jnp.dot(a, b, preferred_element_type=f32)


def dot_split(a_high, a_low, b_high, b_low):
    return dot(a_high, b_high) + (dot(a_low, b_high) + dot(a_high, b_low))


def split_table(table):
    high = table.astype(np.float32).astype(ml_dtypes.bfloat16)
    low = (table - high.astype(np.float64)).astype(np.float32).astype(ml_dtypes.bfloat16)
    return jnp.asarray(high), jnp.asarray(low)


def transforms(length):
    orders = np.concatenate([np.arange(0, length, 2), np.arange(1, length, 2)])
    angle = math.pi / length * (orders[None, :] + 0.5) * np.arange(length)[:, None]
    forward = np.concatenate([np.cos(angle), -np.sin(angle)], axis=1)
    return split_table(forward), split_table(forward.T / length)


def far_memory(x):
    return pltpu.with_memory_space_constraint(x, pltpu.HBM)


def near_core(x):
    return pltpu.with_memory_space_constraint(x, pltpu.VMEM)


def call(body, out_shape, *, grid_spec=None, in_specs=None, out_specs=None, scratch=(), room=16, aliases=None, work=1):
    params = pltpu.CompilerParams(vmem_limit_bytes=room * MIB)
    cost = pl.CostEstimate(flops=work, bytes_accessed=1, transcendentals=0)
    kwargs = dict(out_shape=out_shape, compiler_params=params, cost_estimate=cost)
    if aliases:
        kwargs["input_output_aliases"] = aliases
    if grid_spec is not None:
        return pl.pallas_call(body, grid_spec=grid_spec, **kwargs)
    return pl.pallas_call(body, in_specs=in_specs, out_specs=out_specs, scratch_shapes=list(scratch), **kwargs)


def pack_body(group, slim, chunks, order, me_ref, *rest):
    sources, rest = rest[:3], rest[3:]
    outs, (gated, taps), buffers, sems = rest[:-4], rest[-4:-2], rest[-2], rest[-1]
    part = slim // chunks
    me = me_ref[0]
    low = lax.rem(me, group)
    copies = {}
    for t in order:
        start = pl.multiple_of(jnp.bitwise_xor(me // group, t) * LANES, LANES)
        for a, source in enumerate(sources):
            copies[t, a] = pltpu.make_async_copy(source.at[:, pl.ds(start, LANES)], buffers.at[a, t], sems.at[a, t])
            copies[t, a].start()
    for t in order:
        for a in range(3):
            copies[t, a].wait()
        gated[...] = (buffers[0, t] * buffers[1, t]).T
        taps[...] = buffers[2, t].T
        for e in range(group):
            start = jnp.bitwise_xor(low, e) * slim
            for k in range(chunks):
                rows = pl.ds(pl.multiple_of(start + k * part, 8), part)
                out = outs[(t * group + e) * chunks + k]
                out[0:part, :] = gated[rows, :]
                out[part : 2 * part, :] = taps[rows, :]


def pack(me, key_rows, value_rows, filters, count, chunks):
    length, channels = key_rows.shape
    slim = channels // count
    group = LANES // slim
    steps = count // group
    order = list(range(steps // 2, steps)) + list(range(steps // 2))
    hbm = pl.BlockSpec(memory_space=pltpu.HBM)
    vmem = pl.BlockSpec(memory_space=pltpu.VMEM)
    return call(
        functools.partial(pack_body, group, slim, chunks, order),
        [jax.ShapeDtypeStruct((2 * slim // chunks, length), f32)] * (count * chunks),
        in_specs=[pl.BlockSpec(memory_space=pltpu.SMEM)] + [hbm] * 3,
        out_specs=[vmem] * (count * chunks),
        scratch=[
            pltpu.VMEM((LANES, length), f32),
            pltpu.VMEM((LANES, length), f32),
            pltpu.VMEM((3, steps, length, LANES), f32),
            pltpu.SemaphoreType.DMA((3, steps)),
        ],
        room=8,
    )(me, *(pltpu.with_memory_space_constraint(x, pltpu.HBM) for x in (key_rows, value_rows, filters)))


def spectrum_body(slots, chained, me_ref, fwd_high, fwd_low, *refs):
    arrived, out = refs[: len(slots)], refs[-1]
    double = arrived[0].shape[0]
    rows = jnp.concatenate([ref[...] for ref in arrived], axis=0)
    high, low = halves(rows)
    result = dot_split(high, low, fwd_high[...], fwd_low[...])
    for e, s in enumerate(slots):
        out[jnp.bitwise_xor(me_ref[0], s)] = result[e * double : (e + 1) * double]


def spectrum(me, slots, arrived, forward, count, spectra):
    double, length = arrived[0].shape
    vmem = pl.BlockSpec(memory_space=pltpu.VMEM)
    chained = [] if spectra is None else [spectra]
    return call(
        functools.partial(spectrum_body, slots, len(chained)),
        jax.ShapeDtypeStruct((count, double, 2 * length), f32),
        in_specs=[pl.BlockSpec(memory_space=pltpu.SMEM)] + [vmem] * (2 + len(arrived) + len(chained)),
        out_specs=vmem,
        room=16,
        aliases={3 + len(arrived): 0} if chained else None,
    )(me, *forward, *(arrived if chained else map(far_memory, arrived)), *chained)


def products(count, part, length, spectra, totals):
    lane_steps = length // LANES

    def tile(index, carry):
        group = index // lane_steps
        lane = lax.rem(index, lane_steps)
        sign = jnp.where(lane * 2 < lane_steps, 1.0, -1.0).astype(f32)
        top = pl.ds(pl.multiple_of(group * 8, 8), 8)
        bottom = pl.ds(pl.multiple_of(part + group * 8, 8), 8)
        re = pl.ds(pl.multiple_of(lane * LANES, LANES), LANES)
        im = pl.ds(pl.multiple_of(length + lane * LANES, LANES), LANES)
        gated_re = [spectra[p, top, re] for p in range(count)]
        gated_im = [spectra[p, top, im] for p in range(count)]
        taps_re, taps_im = [], []
        last_re = last_im = None
        for q in range(count):
            now_re, now_im = spectra[q, bottom, re], spectra[q, bottom, im]
            if q == 0:
                taps_re.append(now_re)
                taps_im.append(now_im)
            else:
                taps_re.append(now_re - sign * last_im)
                taps_im.append(now_im + sign * last_re)
            last_re, last_im = now_re, now_im
        gated_sum = [a + b for a, b in zip(gated_re, gated_im)]
        taps_sum = [a + b for a, b in zip(taps_re, taps_im)]
        for i in range(count):
            reals, imags, sums = (
                sum(a[p] * b[i - p] for p in range(1, i + 1)) + a[0] * b[i]
                for a, b in ((gated_re, taps_re), (gated_im, taps_im), (gated_sum, taps_sum))
            )
            totals[i, top, re] = reals - imags
            totals[i, top, im] = sums - reals - imags
        return carry

    lax.fori_loop(0, part // 8 * lane_steps, tile, 0)


def conv_body(late, far, count, me_ref, fwd_high, fwd_low, inv_high, inv_low, *rest):
    arrived, rest = rest[: len(late)], rest[len(late) + 1 :]
    outs, (left, spectra, totals) = rest[: len(far)], rest[len(far) :]
    near = [s for s in range(count) if s not in far]
    me = me_ref[0]
    double, length = arrived[0].shape
    part = double // 2
    rows = jnp.concatenate([ref[...] for ref in arrived], axis=0)
    high, low = halves(rows)
    result = dot_split(high, low, fwd_high[...], fwd_low[...])
    for e, s in enumerate(late):
        spectra[jnp.bitwise_xor(me, s)] = result[e * double : (e + 1) * double]
    products(count, part, length, spectra, totals)
    stacked = jnp.concatenate([totals[jnp.bitwise_xor(me, s)] for s in far], axis=0)
    high, low = halves(stacked)
    result = dot_split(high, low, inv_high[...], inv_low[...])
    for e in range(len(far)):
        outs[e][...] = result[e * part : (e + 1) * part]
    for e, s in enumerate(near):
        left[e * part : (e + 1) * part, :] = totals[jnp.bitwise_xor(me, s)]


def convolve(me, late, far, arrived, spectra, forward, inverse):
    count = spectra.shape[0]
    double, length = arrived[0].shape
    part = double // 2
    vmem = pl.BlockSpec(memory_space=pltpu.VMEM)
    *pieces, left, _ = call(
        functools.partial(conv_body, late, far, count),
        [jax.ShapeDtypeStruct((part, length), f32)] * len(far)
        + [
            jax.ShapeDtypeStruct(((count - len(far)) * part, 2 * length), f32),
            jax.ShapeDtypeStruct(spectra.shape, f32),
        ],
        in_specs=[pl.BlockSpec(memory_space=pltpu.SMEM)] + [vmem] * (5 + len(late)),
        out_specs=[vmem] * (len(far) + 2),
        scratch=[pltpu.VMEM((count, part, 2 * length), f32)],
        room=24,
        aliases={5 + len(late): len(far) + 1},
    )(me, *forward, *inverse, *arrived, spectra)
    return pieces, left


def restore_body(left, inv_high, inv_low, *outs):
    part = outs[0].shape[0]
    high, low = halves(left[...])
    result = dot_split(high, low, inv_high[...], inv_low[...])
    for e, out in enumerate(outs):
        out[...] = result[e * part : (e + 1) * part]


def restore(left, inverse, pieces):
    rows, width = left.shape
    vmem = pl.BlockSpec(memory_space=pltpu.VMEM)
    return call(
        restore_body,
        [jax.ShapeDtypeStruct((rows // pieces, width // 2), f32)] * pieces,
        in_specs=[vmem] * 3,
        out_specs=[vmem] * pieces,
        room=16,
    )(left, *inverse)


def gates_body(count, units, me_ref, query_ref, key_ref, value_ref, skip_ref, *refs):
    outs, (gate_t, direct_t) = refs[:-2], refs[-2:]
    query = query_ref[...]
    gate_t[...] = query.T
    direct_t[...] = (query * (skip_ref[...] * (key_ref[...] * value_ref[...]))).T
    part = gate_t.shape[0] // count
    for u, unit in enumerate(units):
        for e, s in enumerate(unit):
            source = pl.ds(pl.multiple_of(jnp.bitwise_xor(me_ref[0], s) * part, 8), part)
            here = pl.ds(e * part, part)
            outs[2 * u][here, :] = gate_t[source, :]
            outs[2 * u + 1][here, :] = direct_t[source, :]


def gates(me, query_rows, key_rows, value_rows, skip_gain, count, units):
    length, channels = query_rows.shape
    part = channels // count
    vmem = pl.BlockSpec(memory_space=pltpu.VMEM)
    flat = call(
        functools.partial(gates_body, count, units),
        [jax.ShapeDtypeStruct((len(unit) * part, length), f32) for unit in units for _ in range(2)],
        in_specs=[pl.BlockSpec(memory_space=pltpu.SMEM)] + [vmem] * 4,
        out_specs=[vmem] * (2 * len(units)),
        scratch=[pltpu.VMEM((channels, length), f32)] * 2,
        room=16,
        work=80 * 10**9,
    )(me, query_rows, key_rows, value_rows, skip_gain[None, :])
    return [flat[2 * u : 2 * u + 2] for u in range(len(units))]


def mix_body(first, chained, *refs):
    out, whole = refs[-2:]
    *pieces, gate, direct = refs[: len(refs) - 2 - chained]
    part = pieces[0].shape[0]
    for e, piece in enumerate(pieces):
        here = pl.ds(e * part, part)
        mixed = gate[here, :] * piece[...] + direct[here, :]
        out[here, :] = mixed
        whole[pl.ds((first + e) * part, part), :] = mixed


def mix(pieces, gate, direct, first, count, whole):
    part, length = pieces[0].shape
    held = len(pieces)
    vmem = pl.BlockSpec(memory_space=pltpu.VMEM)
    chained = [] if whole is None else [whole]
    return call(
        functools.partial(mix_body, first, len(chained)),
        [jax.ShapeDtypeStruct((held * part, length), f32), jax.ShapeDtypeStruct((count * part, length), f32)],
        in_specs=[vmem] * (held + 2 + len(chained)),
        out_specs=[vmem] * 2,
        room=8,
        aliases={held + 2: 1} if chained else None,
    )(*pieces, *((gate, direct) if chained else (far_memory(gate), far_memory(direct))), *chained)


def cut_body(weight_ref, out_ref):
    out_ref[0] = weight_ref[...]


def cut(out_weight, peers):
    channels, total = out_weight.shape
    width = total // peers
    return call(
        cut_body,
        jax.ShapeDtypeStruct((peers, channels, width), f32),
        grid_spec=pl.GridSpec(
            grid=(peers,),
            in_specs=[pl.BlockSpec((channels, width), lambda o: (0, o))],
            out_specs=pl.BlockSpec((1, channels, width), lambda o: (o, 0, 0)),
        ),
        room=8,
    )(pltpu.with_memory_space_constraint(out_weight, pltpu.HBM))


def weights_body(count, chunks, me_ref, mine_ref, weight_ref, high_ref, low_ref, ordered):
    slim = ordered.shape[0] // count
    part = slim // chunks
    for k in range(chunks):
        for s in range(count):
            start = jnp.bitwise_xor(me_ref[0], s) * slim + k * part
            ordered[pl.ds((k * count + s) * part, part), :] = weight_ref[0, pl.ds(pl.multiple_of(start, 8), part), :]
    high, low = halves(ordered[...].T)
    high_ref[...] = high
    low_ref[...] = low


def weights(me, mine, blocks, count, chunks):
    peers, channels, width = blocks.shape
    result = pl.BlockSpec((width, channels), lambda o, me_ref, mine_ref: (0, o))
    return call(
        functools.partial(weights_body, count, chunks),
        [jax.ShapeDtypeStruct((width, peers * channels), bf16)] * 2,
        grid_spec=pltpu.PrefetchScalarGridSpec(
            num_scalar_prefetch=2,
            grid=(peers,),
            in_specs=[pl.BlockSpec((1, channels, width), lambda o, me_ref, mine_ref: (jnp.bitwise_xor(mine_ref[0], o), 0, 0))],
            out_specs=[result] * 2,
            scratch_shapes=[pltpu.VMEM((channels, width), f32)],
        ),
        room=12,
        work=20 * 10**9,
    )(me, mine, blocks)


def project_body(entries, started, final, *refs):
    count = 1 + max(entry[0] for entry in entries)
    before, refs = refs[:started], refs[started:]
    mixed, (table_high, table_low), rest = refs[:count], refs[count : count + 2], refs[count + 2 :]
    rows = jnp.concatenate([mixed[i][a : a + n, :] for i, a, n, _ in entries], axis=0)
    high, low = halves(rows)
    out = rest[0]
    steps = 4 if final else 1
    span = out.shape[0] // steps
    copies = []
    for r in range(steps):
        here = pl.ds(r * span, span)
        w_high = jnp.concatenate([table_high[here, c : c + n] for _, _, n, c in entries], axis=1)
        w_low = jnp.concatenate([table_low[here, c : c + n] for _, _, n, c in entries], axis=1)
        total = dot_split(w_high, w_low, high, low)
        if started:
            total = total + before[0][here, :]
        if final:
            held, sems = rest[-2:]
            held[here, :] = total
            copies.append(pltpu.make_async_copy(held.at[here, :], out.at[here, :], sems.at[r]))
            copies[-1].start()
        else:
            out[...] = total
    for copy in copies:
        copy.wait()


def project(entries, tables, total=None, final=False, work=1):
    arrays, places = [], []
    for array, *place in entries:
        found = [i for i, other in enumerate(arrays) if other is array]
        if not found:
            arrays.append(array)
        places.append((found[0] if found else len(arrays) - 1, *place))
    length = arrays[0].shape[1]
    high, low = tables
    width = high.shape[0]
    vmem = pl.BlockSpec(memory_space=pltpu.VMEM)
    started = total is not None
    return call(
        functools.partial(project_body, places, started, final),
        jax.ShapeDtypeStruct((width, length), f32),
        in_specs=[vmem] * (len(arrays) + 2 + started),
        out_specs=pl.BlockSpec(memory_space=pltpu.HBM) if final else vmem,
        scratch=[pltpu.VMEM((width, length), f32), pltpu.SemaphoreType.DMA((4,))] if final else [],
        room=16,
        work=work,
    )(*([total] * started), *map(near_core, arrays), high, low)


def swap(x, axis, size, offset):
    return lax.ppermute(x, axis, [(j, j ^ offset) for j in range(size)])


def spread(x, bit):
    found = {0: x}
    for o in range(1, bit):
        found[o] = swap(found[o & (o - 1)], "ch", lax.axis_size("ch"), o & -o)
    return found


def after(value, others):
    return lax.optimization_barrier((value, others))[0]


def per_device(query_rows, key_rows, value_rows, filters, skip_gain, out_weight):
    count = lax.axis_size("seq")
    peers = lax.axis_size("ch")
    length, channels = query_rows.shape
    slim = channels // count
    chunks = max(1, min(CHUNKS, slim // 8))
    width = out_weight.shape[1] // peers
    me = lax.axis_index("seq").astype(jnp.int32).reshape(1)
    mine = lax.axis_index("ch").astype(jnp.int32)
    forward, inverse = transforms(length)

    pieces = pack(me, key_rows, value_rows, filters, count, chunks)
    sent = [pieces[k::chunks] for k in range(chunks)]
    half = count // 2
    near, far = list(range(half)), list(range(half, count))
    arrived = [[None] * count for _ in range(chunks)]
    for k in range(chunks):
        for s in far:
            arrived[k][s] = swap(sent[k][s], "seq", count, s)
        for s in near[1:]:
            piece = sent[k][s] if s < 3 else after(sent[k][s], arrived[k][s - 1])
            arrived[k][s] = swap(piece, "seq", count, s)
        arrived[k][0] = sent[k][0]
    blocks = cut(after(out_weight, sent[0][half]), peers)
    blocks = lax.all_to_all(blocks, "ch", split_axis=0, concat_axis=0, tiled=True)

    part = slim // chunks
    units = [near, far]
    if half // 2 * part % LANES == 0:
        units = [near, far[: half // 2], far[half // 2 :]]
    gated = gates(me, query_rows, key_rows, value_rows, skip_gain, count, units)
    early, late = [near, far[: half // 2]], far[half // 2 :]
    total = None
    tables = None
    for k in range(chunks):
        spectra = None
        for slots in early:
            pieces = [arrived[k][s] for s in slots]
            if spectra is not None:
                spectra, pieces = lax.optimization_barrier((spectra, pieces))
            spectra = spectrum(me, slots, pieces, forward, count, spectra)
        last = [arrived[k][s] for s in late]
        spectra, last, gated = lax.optimization_barrier((spectra, last, gated))
        back = [None] * count
        pieces, left = convolve(me, late, far, last, spectra, forward, inverse)
        for s, piece in zip(far, pieces):
            back[s] = swap(piece, "seq", count, s)
        for s, piece in zip(near, restore(left, inverse, half)):
            back[s] = swap(piece, "seq", count, s) if s else piece
        if tables is None:
            tables = weights(after(me, left), mine.reshape(1), blocks, count, chunks)
        bit = peers // 2
        own, far_own, whole = [], [], None
        last = len(units) - 1
        starts = [unit[0] * part for unit in units]
        sizes = [len(unit) * part for unit in units]

        def entry(array, u, o, row=0):
            return (array, row, sizes[u], o * channels + starts[u])

        for u, unit in enumerate(units):
            pieces = [back[s] for s in unit]
            if u:
                total = project([entry(own[u - 1], u - 1, 0)], tables, total, work=20 * 10**9)
                total, pieces = lax.optimization_barrier((total, pieces))
            alone, whole = mix(pieces, *gated[u], unit[0], count, whole)
            own.append(alone)
            far_own.append(swap(alone, "ch", peers, bit))

    beside = spread(whole, bit)
    across = [spread(after(x, own[last]), bit) for x in far_own[:last]]
    total = project([entry(own[last], last, 0), entry(across[0][0], 0, bit)], tables, total, work=20 * 10**9)
    total = project([(beside[o], 0, channels, o * channels) for o in range(1, bit)], tables, total, work=20 * 10**9)
    if last > 1:
        entries = [entry(across[u][0], u, bit) for u in range(1, last)]
        entries += [entry(across[u][o], u, bit | o) for u in range(last - 1) for o in range(1, bit)]
        total = project(entries, tables, total, work=20 * 10**9)
    total, ending = lax.optimization_barrier((total, far_own[last]))
    ending = spread(ending, bit)
    entries = [entry(ending[0], last, bit)]
    entries += [entry(across[last - 1][o], last - 1, bit | o) for o in range(1, bit)]
    total = project(entries, tables, total)
    total = project([entry(ending[o], last, bit | o) for o in range(1, bit)], tables, total, True)
    return total


def solution(mesh):
    in_specs = (
        P("seq", "ch"),
        P("seq", "ch"),
        P("seq", "ch"),
        P("seq", "ch"),
        P("ch"),
        P("ch", None),
    )
    out_specs = P("ch", "seq")
    return jax.shard_map(
        per_device, mesh=mesh, in_specs=in_specs, out_specs=out_specs, check_vma=False
    )
```

```python
import functools
import math

import jax
import jax.numpy as jnp
import ml_dtypes
import numpy as np
from jax import lax
from jax.experimental import pallas as pl
from jax.experimental.pallas import tpu as pltpu
from jax.sharding import PartitionSpec as P

LANES = 128
MIB = 1024 * 1024
CHUNKS = 1

f32 = jnp.float32
bf16 = jnp.bfloat16


def halves(x):
    high = x.astype(bf16)
    return high, (x - high.astype(f32)).astype(bf16)


def dot(a, b):
    return jnp.dot(a, b, preferred_element_type=f32)


def dot_split(a_high, a_low, b_high, b_low):
    return dot(a_high, b_high) + (dot(a_low, b_high) + dot(a_high, b_low))


def split_table(table):
    high = table.astype(np.float32).astype(ml_dtypes.bfloat16)
    low = (table - high.astype(np.float64)).astype(np.float32).astype(ml_dtypes.bfloat16)
    return jnp.asarray(high), jnp.asarray(low)


def transforms(length):
    orders = np.concatenate([np.arange(0, length, 2), np.arange(1, length, 2)])
    angle = math.pi / length * (orders[None, :] + 0.5) * np.arange(length)[:, None]
    forward = np.concatenate([np.cos(angle), -np.sin(angle)], axis=1)
    return split_table(forward), split_table(forward.T / length)


def far_memory(x):
    return pltpu.with_memory_space_constraint(x, pltpu.HBM)


def near_core(x):
    return pltpu.with_memory_space_constraint(x, pltpu.VMEM)


def call(body, out_shape, *, grid_spec=None, in_specs=None, out_specs=None, scratch=(), room=16, aliases=None, work=1):
    params = pltpu.CompilerParams(vmem_limit_bytes=room * MIB)
    cost = pl.CostEstimate(flops=work, bytes_accessed=1, transcendentals=0)
    kwargs = dict(out_shape=out_shape, compiler_params=params, cost_estimate=cost)
    if aliases:
        kwargs["input_output_aliases"] = aliases
    if grid_spec is not None:
        return pl.pallas_call(body, grid_spec=grid_spec, **kwargs)
    return pl.pallas_call(body, in_specs=in_specs, out_specs=out_specs, scratch_shapes=list(scratch), **kwargs)


def pack_body(group, slim, chunks, order, me_ref, *rest):
    sources, rest = rest[:3], rest[3:]
    outs, (gated, taps), buffers, sems = rest[:-4], rest[-4:-2], rest[-2], rest[-1]
    part = slim // chunks
    me = me_ref[0]
    low = lax.rem(me, group)
    copies = {}
    for t in order:
        start = pl.multiple_of(jnp.bitwise_xor(me // group, t) * LANES, LANES)
        for a, source in enumerate(sources):
            copies[t, a] = pltpu.make_async_copy(source.at[:, pl.ds(start, LANES)], buffers.at[a, t], sems.at[a, t])
            copies[t, a].start()
    for t in order:
        for a in range(3):
            copies[t, a].wait()
        gated[...] = (buffers[0, t] * buffers[1, t]).T
        taps[...] = buffers[2, t].T
        for e in range(group):
            start = jnp.bitwise_xor(low, e) * slim
            for k in range(chunks):
                rows = pl.ds(pl.multiple_of(start + k * part, 8), part)
                out = outs[(t * group + e) * chunks + k]
                out[0:part, :] = gated[rows, :]
                out[part : 2 * part, :] = taps[rows, :]


def pack(me, key_rows, value_rows, filters, count, chunks):
    length, channels = key_rows.shape
    slim = channels // count
    group = LANES // slim
    steps = count // group
    order = list(range(steps // 2, steps)) + list(range(steps // 2))
    hbm = pl.BlockSpec(memory_space=pltpu.HBM)
    vmem = pl.BlockSpec(memory_space=pltpu.VMEM)
    return call(
        functools.partial(pack_body, group, slim, chunks, order),
        [jax.ShapeDtypeStruct((2 * slim // chunks, length), f32)] * (count * chunks),
        in_specs=[pl.BlockSpec(memory_space=pltpu.SMEM)] + [hbm] * 3,
        out_specs=[vmem] * (count * chunks),
        scratch=[
            pltpu.VMEM((LANES, length), f32),
            pltpu.VMEM((LANES, length), f32),
            pltpu.VMEM((3, steps, length, LANES), f32),
            pltpu.SemaphoreType.DMA((3, steps)),
        ],
        room=8,
    )(me, *(pltpu.with_memory_space_constraint(x, pltpu.HBM) for x in (key_rows, value_rows, filters)))


def spectrum_body(slots, chained, me_ref, fwd_high, fwd_low, *refs):
    arrived, out = refs[: len(slots)], refs[-1]
    double = arrived[0].shape[0]
    rows = jnp.concatenate([ref[...] for ref in arrived], axis=0)
    high, low = halves(rows)
    result = dot_split(high, low, fwd_high[...], fwd_low[...])
    for e, s in enumerate(slots):
        out[jnp.bitwise_xor(me_ref[0], s)] = result[e * double : (e + 1) * double]


def spectrum(me, slots, arrived, forward, count, spectra):
    double, length = arrived[0].shape
    vmem = pl.BlockSpec(memory_space=pltpu.VMEM)
    chained = [] if spectra is None else [spectra]
    return call(
        functools.partial(spectrum_body, slots, len(chained)),
        jax.ShapeDtypeStruct((count, double, 2 * length), f32),
        in_specs=[pl.BlockSpec(memory_space=pltpu.SMEM)] + [vmem] * (2 + len(arrived) + len(chained)),
        out_specs=vmem,
        room=16,
        aliases={3 + len(arrived): 0} if chained else None,
    )(me, *forward, *(arrived if chained else map(far_memory, arrived)), *chained)


def products(count, part, length, spectra, totals):
    lane_steps = length // LANES

    def tile(index, carry):
        group = index // lane_steps
        lane = lax.rem(index, lane_steps)
        sign = jnp.where(lane * 2 < lane_steps, 1.0, -1.0).astype(f32)
        top = pl.ds(pl.multiple_of(group * 8, 8), 8)
        bottom = pl.ds(pl.multiple_of(part + group * 8, 8), 8)
        re = pl.ds(pl.multiple_of(lane * LANES, LANES), LANES)
        im = pl.ds(pl.multiple_of(length + lane * LANES, LANES), LANES)
        gated_re = [spectra[p, top, re] for p in range(count)]
        gated_im = [spectra[p, top, im] for p in range(count)]
        taps_re, taps_im = [], []
        last_re = last_im = None
        for q in range(count):
            now_re, now_im = spectra[q, bottom, re], spectra[q, bottom, im]
            if q == 0:
                taps_re.append(now_re)
                taps_im.append(now_im)
            else:
                taps_re.append(now_re - sign * last_im)
                taps_im.append(now_im + sign * last_re)
            last_re, last_im = now_re, now_im
        gated_sum = [a + b for a, b in zip(gated_re, gated_im)]
        taps_sum = [a + b for a, b in zip(taps_re, taps_im)]
        for i in range(count):
            reals, imags, sums = (
                sum(a[p] * b[i - p] for p in range(1, i + 1)) + a[0] * b[i]
                for a, b in ((gated_re, taps_re), (gated_im, taps_im), (gated_sum, taps_sum))
            )
            totals[i, top, re] = reals - imags
            totals[i, top, im] = sums - reals - imags
        return carry

    lax.fori_loop(0, part // 8 * lane_steps, tile, 0)


def conv_body(late, far, count, me_ref, fwd_high, fwd_low, inv_high, inv_low, *rest):
    arrived, rest = rest[: len(late)], rest[len(late) + 1 :]
    outs, (left, spectra, totals) = rest[: len(far)], rest[len(far) :]
    near = [s for s in range(count) if s not in far]
    me = me_ref[0]
    double, length = arrived[0].shape
    part = double // 2
    rows = jnp.concatenate([ref[...] for ref in arrived], axis=0)
    high, low = halves(rows)
    result = dot_split(high, low, fwd_high[...], fwd_low[...])
    for e, s in enumerate(late):
        spectra[jnp.bitwise_xor(me, s)] = result[e * double : (e + 1) * double]
    products(count, part, length, spectra, totals)
    stacked = jnp.concatenate([totals[jnp.bitwise_xor(me, s)] for s in far], axis=0)
    high, low = halves(stacked)
    result = dot_split(high, low, inv_high[...], inv_low[...])
    for e in range(len(far)):
        outs[e][...] = result[e * part : (e + 1) * part]
    for e, s in enumerate(near):
        left[e * part : (e + 1) * part, :] = totals[jnp.bitwise_xor(me, s)]


def convolve(me, late, far, arrived, spectra, forward, inverse):
    count = spectra.shape[0]
    double, length = arrived[0].shape
    part = double // 2
    vmem = pl.BlockSpec(memory_space=pltpu.VMEM)
    *pieces, left, _ = call(
        functools.partial(conv_body, late, far, count),
        [jax.ShapeDtypeStruct((part, length), f32)] * len(far)
        + [
            jax.ShapeDtypeStruct(((count - len(far)) * part, 2 * length), f32),
            jax.ShapeDtypeStruct(spectra.shape, f32),
        ],
        in_specs=[pl.BlockSpec(memory_space=pltpu.SMEM)] + [vmem] * (5 + len(late)),
        out_specs=[vmem] * (len(far) + 2),
        scratch=[pltpu.VMEM((count, part, 2 * length), f32)],
        room=24,
        aliases={5 + len(late): len(far) + 1},
    )(me, *forward, *inverse, *arrived, spectra)
    return pieces, left


def restore_body(left, inv_high, inv_low, *outs):
    part = outs[0].shape[0]
    high, low = halves(left[...])
    result = dot_split(high, low, inv_high[...], inv_low[...])
    for e, out in enumerate(outs):
        out[...] = result[e * part : (e + 1) * part]


def restore(left, inverse, pieces):
    rows, width = left.shape
    vmem = pl.BlockSpec(memory_space=pltpu.VMEM)
    return call(
        restore_body,
        [jax.ShapeDtypeStruct((rows // pieces, width // 2), f32)] * pieces,
        in_specs=[vmem] * 3,
        out_specs=[vmem] * pieces,
        room=16,
    )(left, *inverse)


def gates_body(count, units, me_ref, query_ref, key_ref, value_ref, skip_ref, *refs):
    outs, (gate_t, direct_t) = refs[:-2], refs[-2:]
    query = query_ref[...]
    gate_t[...] = query.T
    direct_t[...] = (query * (skip_ref[...] * (key_ref[...] * value_ref[...]))).T
    part = gate_t.shape[0] // count
    for u, unit in enumerate(units):
        for e, s in enumerate(unit):
            source = pl.ds(pl.multiple_of(jnp.bitwise_xor(me_ref[0], s) * part, 8), part)
            here = pl.ds(e * part, part)
            outs[2 * u][here, :] = gate_t[source, :]
            outs[2 * u + 1][here, :] = direct_t[source, :]


def gates(me, query_rows, key_rows, value_rows, skip_gain, count, units):
    length, channels = query_rows.shape
    part = channels // count
    vmem = pl.BlockSpec(memory_space=pltpu.VMEM)
    flat = call(
        functools.partial(gates_body, count, units),
        [jax.ShapeDtypeStruct((len(unit) * part, length), f32) for unit in units for _ in range(2)],
        in_specs=[pl.BlockSpec(memory_space=pltpu.SMEM)] + [vmem] * 4,
        out_specs=[vmem] * (2 * len(units)),
        scratch=[pltpu.VMEM((channels, length), f32)] * 2,
        room=16,
        work=80 * 10**9,
    )(me, query_rows, key_rows, value_rows, skip_gain[None, :])
    return [flat[2 * u : 2 * u + 2] for u in range(len(units))]


def mix_body(first, chained, *refs):
    out, whole = refs[-2:]
    *pieces, gate, direct = refs[: len(refs) - 2 - chained]
    part = pieces[0].shape[0]
    for e, piece in enumerate(pieces):
        here = pl.ds(e * part, part)
        mixed = gate[here, :] * piece[...] + direct[here, :]
        out[here, :] = mixed
        whole[pl.ds((first + e) * part, part), :] = mixed


def mix(pieces, gate, direct, first, count, whole):
    part, length = pieces[0].shape
    held = len(pieces)
    vmem = pl.BlockSpec(memory_space=pltpu.VMEM)
    chained = [] if whole is None else [whole]
    return call(
        functools.partial(mix_body, first, len(chained)),
        [jax.ShapeDtypeStruct((held * part, length), f32), jax.ShapeDtypeStruct((count * part, length), f32)],
        in_specs=[vmem] * (held + 2 + len(chained)),
        out_specs=[vmem] * 2,
        room=8,
        aliases={held + 2: 1} if chained else None,
    )(*pieces, *((gate, direct) if chained else (far_memory(gate), far_memory(direct))), *chained)


def cut_body(pieces, weight_ref, out_ref, sems):
    peers, channels, width = out_ref.shape
    span = channels // pieces
    copies = []
    for o in range(peers):
        for r in range(pieces):
            rows = pl.ds(r * span, span)
            source = weight_ref.at[rows, pl.ds(o * width, width)]
            copies.append(pltpu.make_async_copy(source, out_ref.at[o, rows, :], sems.at[o, r]))
            copies[-1].start()
    for copy in copies:
        copy.wait()


def cut(out_weight, peers, pieces=4):
    channels, total = out_weight.shape
    hbm = pl.BlockSpec(memory_space=pltpu.HBM)
    return call(
        functools.partial(cut_body, pieces),
        jax.ShapeDtypeStruct((peers, channels, total // peers), f32),
        in_specs=[hbm],
        out_specs=hbm,
        scratch=[pltpu.SemaphoreType.DMA((peers, pieces))],
        room=8,
    )(pltpu.with_memory_space_constraint(out_weight, pltpu.HBM))


def weights_body(count, chunks, me_ref, mine_ref, weight_ref, high_ref, low_ref, ordered):
    slim = ordered.shape[0] // count
    part = slim // chunks
    for k in range(chunks):
        for s in range(count):
            start = jnp.bitwise_xor(me_ref[0], s) * slim + k * part
            ordered[pl.ds((k * count + s) * part, part), :] = weight_ref[0, pl.ds(pl.multiple_of(start, 8), part), :]
    high, low = halves(ordered[...].T)
    high_ref[...] = high
    low_ref[...] = low


def weights(me, mine, blocks, count, chunks):
    peers, channels, width = blocks.shape
    result = pl.BlockSpec((width, channels), lambda o, me_ref, mine_ref: (0, o))
    return call(
        functools.partial(weights_body, count, chunks),
        [jax.ShapeDtypeStruct((width, peers * channels), bf16)] * 2,
        grid_spec=pltpu.PrefetchScalarGridSpec(
            num_scalar_prefetch=2,
            grid=(peers,),
            in_specs=[pl.BlockSpec((1, channels, width), lambda o, me_ref, mine_ref: (jnp.bitwise_xor(mine_ref[0], o), 0, 0))],
            out_specs=[result] * 2,
            scratch_shapes=[pltpu.VMEM((channels, width), f32)],
        ),
        room=12,
        work=20 * 10**9,
    )(me, mine, blocks)


def project_body(entries, started, final, *refs):
    count = 1 + max(entry[0] for entry in entries)
    before, refs = refs[:started], refs[started:]
    mixed, (table_high, table_low), rest = refs[:count], refs[count : count + 2], refs[count + 2 :]
    rows = jnp.concatenate([mixed[i][a : a + n, :] for i, a, n, _ in entries], axis=0)
    high, low = halves(rows)
    out = rest[0]
    steps = 4 if final else 1
    span = out.shape[0] // steps
    copies = []
    for r in range(steps):
        here = pl.ds(r * span, span)
        w_high = jnp.concatenate([table_high[here, c : c + n] for _, _, n, c in entries], axis=1)
        w_low = jnp.concatenate([table_low[here, c : c + n] for _, _, n, c in entries], axis=1)
        total = dot_split(w_high, w_low, high, low)
        if started:
            total = total + before[0][here, :]
        if final:
            held, sems = rest[-2:]
            held[here, :] = total
            copies.append(pltpu.make_async_copy(held.at[here, :], out.at[here, :], sems.at[r]))
            copies[-1].start()
        else:
            out[...] = total
    for copy in copies:
        copy.wait()


def project(entries, tables, total=None, final=False, work=1):
    arrays, places = [], []
    for array, *place in entries:
        found = [i for i, other in enumerate(arrays) if other is array]
        if not found:
            arrays.append(array)
        places.append((found[0] if found else len(arrays) - 1, *place))
    length = arrays[0].shape[1]
    high, low = tables
    width = high.shape[0]
    vmem = pl.BlockSpec(memory_space=pltpu.VMEM)
    started = total is not None
    return call(
        functools.partial(project_body, places, started, final),
        jax.ShapeDtypeStruct((width, length), f32),
        in_specs=[vmem] * (len(arrays) + 2 + started),
        out_specs=pl.BlockSpec(memory_space=pltpu.HBM) if final else vmem,
        scratch=[pltpu.VMEM((width, length), f32), pltpu.SemaphoreType.DMA((4,))] if final else [],
        room=16,
        work=work,
    )(*([total] * started), *map(near_core, arrays), high, low)


def swap(x, axis, size, offset):
    return lax.ppermute(x, axis, [(j, j ^ offset) for j in range(size)])


def spread(x, bit):
    found = {0: x}
    for o in range(1, bit):
        found[o] = swap(found[o & (o - 1)], "ch", lax.axis_size("ch"), o & -o)
    return found


def after(value, others):
    return lax.optimization_barrier((value, others))[0]


def per_device(query_rows, key_rows, value_rows, filters, skip_gain, out_weight):
    count = lax.axis_size("seq")
    peers = lax.axis_size("ch")
    length, channels = query_rows.shape
    slim = channels // count
    chunks = max(1, min(CHUNKS, slim // 8))
    width = out_weight.shape[1] // peers
    me = lax.axis_index("seq").astype(jnp.int32).reshape(1)
    mine = lax.axis_index("ch").astype(jnp.int32)
    forward, inverse = transforms(length)

    pieces = pack(me, key_rows, value_rows, filters, count, chunks)
    sent = [pieces[k::chunks] for k in range(chunks)]
    half = count // 2
    near, far = list(range(half)), list(range(half, count))
    arrived = [[None] * count for _ in range(chunks)]
    for k in range(chunks):
        for s in far:
            arrived[k][s] = swap(sent[k][s], "seq", count, s)
        for s in near[1:]:
            piece = sent[k][s] if s < 3 else after(sent[k][s], arrived[k][s - 1])
            arrived[k][s] = swap(piece, "seq", count, s)
        arrived[k][0] = sent[k][0]
    blocks = cut(after(out_weight, sent[0][half]), peers)
    blocks = lax.all_to_all(blocks, "ch", split_axis=0, concat_axis=0, tiled=True)

    part = slim // chunks
    units = [near, far]
    if half // 2 * part % LANES == 0:
        units = [near, far[: half // 2], far[half // 2 :]]
    gated = gates(me, query_rows, key_rows, value_rows, skip_gain, count, units)
    early, late = [near, far[: half // 2]], far[half // 2 :]
    total = None
    tables = None
    for k in range(chunks):
        spectra = None
        for slots in early:
            pieces = [arrived[k][s] for s in slots]
            if spectra is not None:
                spectra, pieces = lax.optimization_barrier((spectra, pieces))
            spectra = spectrum(me, slots, pieces, forward, count, spectra)
        last = [arrived[k][s] for s in late]
        spectra, last, gated = lax.optimization_barrier((spectra, last, gated))
        back = [None] * count
        pieces, left = convolve(me, late, far, last, spectra, forward, inverse)
        for s, piece in zip(far, pieces):
            back[s] = swap(piece, "seq", count, s)
        for s, piece in zip(near, restore(left, inverse, half)):
            back[s] = swap(piece, "seq", count, s) if s else piece
        if tables is None:
            tables = weights(after(me, left), mine.reshape(1), blocks, count, chunks)
        bit = peers // 2
        own, far_own, whole = [], [], None
        last = len(units) - 1
        starts = [unit[0] * part for unit in units]
        sizes = [len(unit) * part for unit in units]

        def entry(array, u, o, row=0):
            return (array, row, sizes[u], o * channels + starts[u])

        for u, unit in enumerate(units):
            pieces = [back[s] for s in unit]
            if u:
                total = project([entry(own[u - 1], u - 1, 0)], tables, total, work=20 * 10**9)
                total, pieces = lax.optimization_barrier((total, pieces))
            alone, whole = mix(pieces, *gated[u], unit[0], count, whole)
            own.append(alone)
            far_own.append(swap(alone, "ch", peers, bit))

    beside = spread(whole, bit)
    across = [spread(after(x, own[last]), bit) for x in far_own[:last]]
    total = project([entry(own[last], last, 0), entry(across[0][0], 0, bit)], tables, total, work=20 * 10**9)
    total = project([(beside[o], 0, channels, o * channels) for o in range(1, bit)], tables, total, work=20 * 10**9)
    if last > 1:
        entries = [entry(across[u][0], u, bit) for u in range(1, last)]
        entries += [entry(across[u][o], u, bit | o) for u in range(last - 1) for o in range(1, bit)]
        total = project(entries, tables, total, work=20 * 10**9)
    total, ending = lax.optimization_barrier((total, far_own[last]))
    ending = spread(ending, bit)
    entries = [entry(ending[0], last, bit)]
    entries += [entry(across[last - 1][o], last - 1, bit | o) for o in range(1, bit)]
    total = project(entries, tables, total)
    total = project([entry(ending[o], last, bit | o) for o in range(1, bit)], tables, total, True)
    return total


def solution(mesh):
    in_specs = (
        P("seq", "ch"),
        P("seq", "ch"),
        P("seq", "ch"),
        P("seq", "ch"),
        P("ch"),
        P("ch", None),
    )
    out_specs = P("ch", "seq")
    return jax.shard_map(
        per_device, mesh=mesh, in_specs=in_specs, out_specs=out_specs, check_vma=False
    )
```
